256 devices in a mesh: hist: 32 (over z, x), row: 8 (over y, core).
Axes of the slice: x: 4, y: 4, z: 8, core: 2. Of those that a mesh axis runs over, the one named last changes fastest.
Arguments:
- row_less: float32 [2, 384, 1024], P(None, 'hist'), may hold values from -40 to 40
- row_great: float32 [2, 384, 1024], P(None, 'hist'), may hold values from -5 to 5
- coupling: float32 [32, 32], replicated, may hold values from -1 to 1
- damping: float32 [384, 32], P('hist'), may hold values from 0.2 to 1, as said below
- phases: float32 [384, 32], P('hist'), may hold values from -3.140625 to 3.140625
- lesser_hist: bfloat16 [2, 384, 384, 1024], P(None, 'row', 'hist'), may hold values from -5 to 5
- advanced_hist: bfloat16 [2, 384, 384, 1024], P(None, 'row', 'hist'), may hold values from -5 to 5
- retarded_hist: bfloat16 [2, 384, 384, 1024], P(None, 'row', 'hist'), may hold values from -5 to 5
Outputs:
- stepped_row: float32 [2, 384, 1024], P(None, 'hist')
- column_term: float32 [2, 384, 1024], P(None, 'row')
The draws below stay inside these ranges and needn't reach their ends.
Inputs may be any that keep to these rules, and one draw needn't show every extreme that they name: `damping`: one-step magnitudes.
All inputs are finite; a program needn't handle non-finite values.
Results may differ from the reference program's by a relative error of at most 0.0029.
Values may be sent and summed in bfloat16 or wider, within the bound.
A program may use at most 128 MiB of HBM per device.

```python
import math
import jax
import jax.numpy as jnp
from jax import lax

NB = 32
TP = 12
PAST_TIME_SLICES = 384
N_HIST = 32


def draw_row_less(key, part):
    key = jax.random.fold_in(key, 5)
    key_cols, key_base = jax.random.split(key, 2)
    col_scale = jnp.exp(jax.random.uniform(key_cols, (NB * NB,), jnp.float32, math.log(0.4), math.log(4.0)))
    base = jnp.clip(jax.random.normal(key_base, (2, PAST_TIME_SLICES, NB * NB), jnp.float32), -3.5, 3.5)
    values = base * col_scale[None, None, :]
    return values.astype(jnp.float32)


def draw_damping(key, part):
    key = jax.random.fold_in(key, 11)
    key_fast, key_len, key_rough, random_seed_slot, key_depth = jax.random.split(key, 5)
    fast_percent = 50
    fast = jax.random.randint(key_fast, (NB,), 0, 100) < fast_percent
    fast_len = jax.random.uniform(key_len, (NB,), jnp.float32, 15.0, 25.0)
    slow_len = jax.random.uniform(key_len, (NB,), jnp.float32, 3.0 * PAST_TIME_SLICES, 5.0 * PAST_TIME_SLICES)
    length = jnp.where(fast, fast_len, slow_len)
    rough = jax.random.uniform(key_rough, (PAST_TIME_SLICES, NB), jnp.float32, 0.5, 2.0)
    attenuation_speed = jnp.exp(-rough / length[None, :])
    spike_instant = jax.random.randint(random_seed_slot, (3,), 0, PAST_TIME_SLICES)
    memory_length = jax.random.uniform(key_depth, (3, NB), jnp.float32, 0.65, 0.85)
    spike_arrival = jnp.arange(PAST_TIME_SLICES, dtype=jnp.int32)[:, None] == spike_instant[None, :]
    spike_occurrence = jnp.prod(jnp.where(spike_arrival[:, :, None], memory_length[None, :, :], 1.0), axis=1)
    return (attenuation_speed * spike_occurrence).astype(jnp.float32)


def shard_levels(key, shape, cuts, low, top_value):
    factor_of, own = 1.0, jax.random.fold_in(key, 6)
    for axis_at, blocks in cuts:
        heights = jnp.exp(jax.random.uniform(jax.random.fold_in(own, axis_at), (blocks,), jnp.float32, low / len(cuts), top_value / len(cuts)))
        factor_of = factor_of * jnp.repeat(heights, shape[axis_at] // blocks).reshape([-1 if axis == axis_at else 1 for axis in range(len(shape))])
    return factor_of


def noise(stream_key, dims, deviation, limit, shards=(), held_as=jnp.bfloat16):
    result = deviation * jax.random.normal(stream_key, dims, jnp.float32)
    if shards:
        result = result * shard_levels(stream_key, dims, shards, -0.22, 0.18)
    return jnp.clip(result, -limit, limit).astype(held_as)


def setup_inputs(seed: int = 0) -> dict:
    key_of = jax.random.split(jax.random.key(seed), 9)
    row_less = draw_row_less(jax.random.fold_in(key_of[8], 71), 0)
    row_great = noise(key_of[1], (2, PAST_TIME_SLICES, NB * NB), 1.0, 5.0, ((1, 32),), jnp.float32)
    coupling = noise(key_of[2], (NB, NB), NB ** -0.5, 1.0, (), jnp.float32)
    damping = draw_damping(jax.random.fold_in(key_of[8], 71), 0)
    phases = jnp.clip(jax.random.uniform(key_of[4], (PAST_TIME_SLICES, NB), jnp.float32, -3.140625, 3.140625), -3.140625, 3.140625)
    lesser_hist = noise(key_of[5], (2, PAST_TIME_SLICES, PAST_TIME_SLICES, NB * NB), 1.0, 5.0, ((1, 8), (2, 32)))
    advanced_hist = noise(key_of[6], (2, PAST_TIME_SLICES, PAST_TIME_SLICES, NB * NB), 1.0, 5.0, ((1, 8), (2, 32)))
    retarded_hist = noise(key_of[7], (2, PAST_TIME_SLICES, PAST_TIME_SLICES, NB * NB), 1.0, 5.0, ((1, 8), (2, 32)))
    return {"row_less": row_less, "row_great": row_great, "coupling": coupling, "damping": damping, "phases": phases, "lesser_hist": lesser_hist, "advanced_hist": advanced_hist, "retarded_hist": retarded_hist}


def self_energy(row_less, row_great, coupling):
    steps_here = row_less.shape[1]
    bands = coupling.shape[0]
    less_real = row_less[0].reshape(steps_here, bands, bands)
    less_imag = row_less[1].reshape(steps_here, bands, bands)
    great_real = row_great[0].reshape(steps_here, bands, bands)
    great_imag = row_great[1].reshape(steps_here, bands, bands)
    polar_real = -(less_real * great_real + less_imag * great_imag)
    polar_imag = -(less_imag * great_real - less_real * great_imag)
    highest = lax.Precision.HIGHEST

    def sandwich(polar):
        partial_value = jnp.einsum('ik,skl->sil', coupling, polar, precision=highest)
        return jnp.einsum('sil,jl->sij', partial_value, coupling, precision=highest)
    screen_real = sandwich(polar_real)
    screen_imag = sandwich(polar_imag)
    sigma_less = jnp.stack([less_real * screen_real - less_imag * screen_imag, less_real * screen_imag + less_imag * screen_real])
    sigma_great = jnp.stack([great_real * screen_real + great_imag * screen_imag, great_imag * screen_real - great_real * screen_imag])
    return ((sigma_great - sigma_less).astype(jnp.bfloat16), sigma_less.astype(jnp.bfloat16))

def reference(row_less, row_great, coupling, damping, phases, lesser_hist, advanced_hist, retarded_hist):
    weight = float(PAST_TIME_SLICES * NB) ** (-0.5)
    sigma_ret, sigma_less = self_energy(row_less, row_great, coupling)
    ret_wide = sigma_ret.astype(jnp.float32)
    less_wide = sigma_less.astype(jnp.float32)
    positions = jnp.arange(PAST_TIME_SLICES, dtype=jnp.int32)

    def contract_row(sigma, hist):
        return jnp.einsum('sik,stkj->tij', sigma, hist)

    def row_block(block_index):
        offset = (block_index * TP).astype(jnp.int32)
        lesser = lax.dynamic_slice_in_dim(lesser_hist, offset, TP, 2).astype(jnp.float32).reshape(2, PAST_TIME_SLICES, TP, NB, NB)
        advanced = lax.dynamic_slice_in_dim(advanced_hist, offset, TP, 2).astype(jnp.float32).reshape(2, PAST_TIME_SLICES, TP, NB, NB)
        target_steps = offset + jnp.arange(TP, dtype=jnp.int32)
        causal = positions[:, None] <= target_steps[None, :]
        advanced = jnp.where(causal[None, :, :, None, None], advanced, jnp.zeros((), jnp.float32))
        real_part = contract_row(ret_wide[0], lesser[0]) - contract_row(ret_wide[1], lesser[1]) + contract_row(less_wide[0], advanced[0]) - contract_row(less_wide[1], advanced[1])
        imag_part = contract_row(ret_wide[0], lesser[1]) + contract_row(ret_wide[1], lesser[0]) + contract_row(less_wide[0], advanced[1]) + contract_row(less_wide[1], advanced[0])
        return weight * jnp.stack([real_part, imag_part])
    blocks = lax.map(row_block, jnp.arange(N_HIST, dtype=jnp.int32))
    collision = blocks.transpose(1, 0, 2, 3, 4).reshape(2, PAST_TIME_SLICES, NB * NB)

    def contract_column(hist, sigma):
        return jnp.einsum('tsik,sjk->tij', hist, sigma)

    def column_block(block_index):
        offset = (block_index * TP).astype(jnp.int32)
        retarded = lax.dynamic_slice_in_dim(retarded_hist, offset, TP, 1).astype(jnp.float32).reshape(2, TP, PAST_TIME_SLICES, NB, NB)
        later_steps = offset + jnp.arange(TP, dtype=jnp.int32)
        causal = positions[None, :] <= later_steps[:, None]
        retarded = jnp.where(causal[None, :, :, None, None], retarded, jnp.zeros((), jnp.float32))
        real_part = -(contract_column(retarded[0], less_wide[0]) + contract_column(retarded[1], less_wide[1]))
        imag_part = -(contract_column(retarded[1], less_wide[0]) - contract_column(retarded[0], less_wide[1]))
        return weight * jnp.stack([real_part, imag_part])
    column_blocks = lax.map(column_block, jnp.arange(N_HIST, dtype=jnp.int32))
    column_term = column_blocks.transpose(1, 0, 2, 3, 4).reshape(2, PAST_TIME_SLICES, NB * NB)
    log_rate = jnp.log(damping)
    summed_log = jnp.cumsum(log_rate[::-1], axis=0)[::-1]
    summed_phase = jnp.cumsum(phases[::-1], axis=0)[::-1]
    magnitude = jnp.exp(summed_log)
    factor_real = jnp.repeat(magnitude * jnp.cos(summed_phase), NB, axis=1)
    factor_imag = jnp.repeat(-magnitude * jnp.sin(summed_phase), NB, axis=1)
    sum_real = row_less[0] + collision[0]
    sum_imag = row_less[1] + collision[1]
    stepped_real = factor_real * sum_real - factor_imag * sum_imag
    stepped_imag = factor_real * sum_imag + factor_imag * sum_real
    squares = jnp.sum(stepped_real * stepped_real) + jnp.sum(stepped_imag * stepped_imag)
    norm_scale = jnp.sqrt(squares / (2 * PAST_TIME_SLICES * NB * NB) + 1e-06)
    stepped_row = jnp.stack([stepped_real, stepped_imag]) / norm_scale
    return (stepped_row, column_term)
```

```python
import functools

import jax
import jax.numpy as jnp
import numpy as np
from jax import lax
from jax.experimental import pallas as pl
from jax.experimental.pallas import tpu as pltpu
from jax.sharding import PartitionSpec as P

MESH = pl.DeviceIdType.MESH
F32 = jnp.float32
BF16 = jnp.bfloat16
HIGHEST = lax.Precision.HIGHEST
NX = 4
NZ = 8
NR = 8
TP = 12
TR = 48
OWNERS = 6
LANES_TO_LANES = (((1,), (1,)), ((), ()))


def lane_order():
    one = np.zeros((TP * 32, 4 * 128), np.float32)
    two = np.zeros((NX * 128, 8 * TR), np.float32)
    for s in range(TP):
        for c in range(8):
            for q in range(4):
                one[s * 32 + 4 * c + q, q * 128 + c * TP + s] = 1
            for x in range(NX):
                two[x * 128 + c * TP + s, c * TR + x * TP + s] = 1
    three = np.zeros((128, 128), np.float32)
    for q in range(4):
        for a in range(4):
            for c in range(8):
                three[q * 32 + a * 8 + c, q * 32 + 4 * c + a] = 1
    return one, two, three


def body(
    x_hbm, y_hbm, c_hbm, damp_hbm, phase_hbm, les_hbm, adv_hbm, ret_hbm, one_hbm, two_hbm, three_hbm,
    out_ref, col_ref,
    xv, yv, cv, dampv, phasev, lesv, advv, retv, onev, twov, threev,
    sig_own, sig_all, bmat, col_acc, col_send, col_x, colz_send, col_z, col_own, col_all,
    lmat, fpart, rs_buf, ag_buf, tot_x, tot_z, nrm_x, nrm_z, facv, stepv,
    load_sem, send_sem, recv_sem,
):
    h = lax.axis_index("hist")
    r = lax.axis_index("row")
    z, x = h // NX, h % NX
    dz = (z - r + NZ) % NZ
    early = z <= r
    late = z >= r

    def at_x(d):
        return {"hist": z * NX + (x + d) % NX}

    def at_z(d):
        return {"hist": ((z + d + NZ) % NZ) * NX + x}

    def at_r(d):
        return {"row": (r + d) % NR}

    counts = {"send": 0, "recv": 0}
    pending = []

    def slots(kind, n):
        first = counts[kind]
        counts[kind] += n
        return first

    def copy(src, dst, send, recv, device):
        return pltpu.make_async_remote_copy(
            src_ref=src, dst_ref=dst, send_sem=send_sem.at[send], recv_sem=recv_sem.at[recv],
            device_id=device, device_id_type=MESH,
        )

    def start(cond, *args):
        if cond is None:
            copy(*args).start()
        else:
            @pl.when(cond)
            def _():
                copy(*args).start()
        pending.append((cond, args))

    def arrived(ref, recv):
        copy(ref, ref, 0, recv, at_x(1)).wait_recv()

    loads = []
    for src, dst in (
        (c_hbm, cv), (x_hbm, xv), (y_hbm, yv), (damp_hbm, dampv), (phase_hbm, phasev),
        (one_hbm, onev), (two_hbm, twov), (three_hbm, threev), (ret_hbm, retv), (les_hbm, lesv), (adv_hbm, advv),
    ):
        loads.append(pltpu.make_async_copy(src, dst, load_sem.at[len(loads)]))
        loads[-1].start()
    (c_load, x_load, y_load, damp_load, phase_load, one_load, two_load, three_load, ret_load, les_load, adv_load) = loads

    barrier = pltpu.get_barrier_semaphore()
    for d in range(1, NX):
        pl.semaphore_signal(barrier, inc=1, device_id=at_x(d), device_id_type=MESH)
    for d in range(1, NZ):
        pl.semaphore_signal(barrier, inc=1, device_id=at_z(d), device_id_type=MESH)
    for d in range(1, NR):
        pl.semaphore_signal(barrier, inc=1, device_id=at_r(d), device_id_type=MESH)

    lane8 = lax.broadcasted_iota(jnp.int32, (8, 128), 1) // 32

    def by_group(parts):
        mask = lane8.reshape((1,) * (parts[0].ndim - 2) + (8, 128))
        out = parts[0]
        for g in range(1, 4):
            out = jnp.where(mask == g, parts[g], out)
        return out

    def rolled(a):
        flat = a.reshape(-1, 128)
        return [a] + [pltpu.roll(flat, 32 * d, 1).reshape(a.shape) for d in range(1, 4)]

    c_load.wait()
    coup = cv[...]
    wide = jnp.concatenate([coup] * 4, axis=1)
    square = jnp.concatenate([wide] * 4, axis=0)
    same = (
        lax.broadcasted_iota(jnp.int32, (128, 128), 0) // 32
        == lax.broadcasted_iota(jnp.int32, (128, 128), 1) // 32
    )
    right = jnp.where(same, square, 0.0)
    rows4 = [cv[pl.ds(g, 8, stride=4), :] for g in range(4)]
    col_of = [[jnp.broadcast_to(rows4[g][:, k : k + 1], (8, 128)) for k in range(32)] for g in range(4)]

    x_load.wait()
    y_load.wait()

    def part(ref, p):
        return ref[pl.ds(p, TP * 8, stride=2), :]

    xr, xi, yr, yi = part(xv, 0), part(xv, 1), part(yv, 0), part(yv, 1)
    polar = jnp.concatenate([-(xr * yr + xi * yi), -(xi * yr - xr * yi)], axis=0)
    half = lax.dot_general(polar, right, LANES_TO_LANES, precision=HIGHEST, preferred_element_type=F32)
    half = half.reshape(2 * TP, 8, 128)
    half_d = rolled(half)
    screen = jnp.zeros((2 * TP, 8, 128), F32)
    for d in range(4):
        for c in range(8):
            factor = by_group([col_of[g][4 * c + (g - d) % 4] for g in range(4)])
            screen = screen + factor[None] * half_d[d][:, c : c + 1, :]
    sr, si = screen[:TP], screen[TP:]
    xr, xi, yr, yi = (a.reshape(TP, 8, 128) for a in (xr, xi, yr, yi))
    less = (xr * sr - xi * si, xr * si + xi * sr)
    great = (yr * sr + yi * si, yi * sr - yr * si)
    ret = (great[0] - less[0], great[1] - less[1])
    less_d = [rolled(a) for a in less]
    for a, pair in enumerate(([rolled(v) for v in ret], less_d)):
        for p in range(2):
            for m in range(3):
                block = jnp.concatenate(
                    [by_group([pair[p][(g - b) % 4][4 * m + g] for g in range(4)]) for b in range(4)], axis=0
                )
                sig_own[a, pl.ds(p * 32, 32), pl.ds(m * 128, 128)] = block.astype(BF16)

    damp_load.wait()
    phase_load.wait()
    logs = jnp.concatenate([jnp.log(dampv[...]), phasev[...]], axis=1)
    tot = jnp.sum(logs, axis=0, keepdims=True)
    tot = jnp.concatenate([tot, jnp.zeros((1, 64), F32)], axis=1)
    tot_x[x] = jnp.broadcast_to(tot, (8, 128))

    pl.semaphore_wait(barrier, (NX - 1) + (NZ - 1) + (NR - 1))

    source = dz == 0
    up = (dz == 1) | (dz == 2) | (dz == 3)
    down = (dz == 7) | (dz == 6)
    z_send, z_recv = slots("send", 4), slots("recv", 2)
    f_send = slots("send", 4)
    sx_send, sx_recv = slots("send", 6), slots("recv", 6)
    for a in range(2):
        start(source, sig_own.at[a], sig_all.at[a, x], z_send + 2 * a, z_recv + a, at_z(1))
        start(source, sig_own.at[a], sig_all.at[a, x], z_send + 2 * a + 1, z_recv + a, at_z(-1))

    @pl.when(source)
    def _():
        sig_all[:, x] = sig_own[...]

    tx_send, tx_recv = slots("send", 3), slots("recv", 3)
    for d in range(1, NX):
        start(None, tot_x.at[x], tot_x.at[x], tx_send + d - 1, tx_recv + d - 1, at_x(d))

    @pl.when(early)
    def _():
        def square_of(p, s):
            rows = []
            for g in range(4):
                for b in range(4):
                    rows.append(jnp.where(lane8 == g, less_d[p][(g - b) % 4][s], 0.0))
            return jnp.concatenate(rows, axis=0)

        for s in range(TP):
            b0, b1 = square_of(0, s), square_of(1, s)
            bmat[s, pl.ds(0, 128), pl.ds(0, 128)] = b0.astype(BF16)
            bmat[s, pl.ds(0, 128), pl.ds(128, 128)] = b1.astype(BF16)
            bmat[s, pl.ds(128, 128), pl.ds(0, 128)] = (-b1).astype(BF16)
            bmat[s, pl.ds(128, 128), pl.ds(128, 128)] = b0.astype(BF16)

    for a in range(2):
        @pl.when(jnp.logical_not(source))
        def _():
            arrived(sig_own.at[a], z_recv + a)

        start(up, sig_all.at[a, x], sig_all.at[a, x], f_send + 2 * a, z_recv + a, at_z(1))
        start(down, sig_all.at[a, x], sig_all.at[a, x], f_send + 2 * a + 1, z_recv + a, at_z(-1))
        for d in range(1, NX):
            start(
                None if a == 0 else late, sig_all.at[a, x], sig_all.at[a, x],
                sx_send + 3 * a + d - 1, sx_recv + 3 * a + d - 1, at_x(d),
            )

    tz_send, tz_recv = slots("send", 7), slots("recv", 7)
    for d in range(1, NX):
        arrived(tot_x.at[0], tx_recv + d - 1)
    tot_z[z] = tot_x[0] + tot_x[1] + tot_x[2] + tot_x[3]
    for d in range(1, NZ):
        start(None, tot_z.at[z], tot_z.at[z], tz_send + d - 1, tz_recv + d - 1, at_z(d))

    weight = float(NX * NZ * TP * 32) ** -0.5
    ret_load.wait()
    three_load.wait()
    cx_send, cx_recv = slots("send", 3), slots("recv", 3)

    @pl.when(early)
    def _():
        t_row = lax.broadcasted_iota(jnp.int32, (TR, 128), 0)
        col_acc[...] = jnp.zeros_like(col_acc)

        def step(s, carry):
            keep = t_row >= h * TP + s - r * TR
            rows = [
                jnp.concatenate(
                    [jnp.where(keep, retv[p, s, :, pl.ds(c * 128, 128)], jnp.zeros((), BF16)) for p in range(2)], axis=1
                )
                for c in range(8)
            ]
            col_acc[...] += lax.dot_general(
                jnp.concatenate(rows, axis=0), bmat[s], LANES_TO_LANES, preferred_element_type=F32
            )
            return carry

        lax.fori_loop(0, TP, step, 0)
        for c in range(8):
            for po in range(2):
                value = (col_acc[pl.ds(c * TR, TR), pl.ds(po * 128, 128)] * -weight).astype(BF16)
                value = jnp.dot(value, threev[...], preferred_element_type=F32)
                col_send[c // 2, pl.ds(((c % 2) * 2 + po) * TR, TR), :] = value.astype(BF16)

    for d in range(1, NX):
        start(early, col_send.at[(x + d) % NX], col_x.at[d - 1], cx_send + d - 1, cx_recv + d - 1, at_x(d))

    one_load.wait()
    two_load.wait()

    def left_matrix(a):
        blocks = [
            jnp.dot(sig_all[a, j], onev[...], preferred_element_type=F32).astype(BF16) for j in range(NX)
        ]
        parts = []
        for p in range(2):
            gathered = jnp.concatenate(
                [
                    jnp.concatenate([b[p * 32 : p * 32 + 32, q * 128 : q * 128 + 128] for b in blocks], axis=1)
                    for q in range(4)
                ],
                axis=0,
            )
            parts.append(jnp.dot(gathered, twov[...], preferred_element_type=F32))
        lmat[pl.ds(0, 128), pl.ds(0, 384)] = parts[0].astype(BF16)
        lmat[pl.ds(0, 128), pl.ds(384, 384)] = (-parts[1]).astype(BF16)
        lmat[pl.ds(128, 128), pl.ds(0, 384)] = parts[1].astype(BF16)
        lmat[pl.ds(128, 128), pl.ds(384, 384)] = parts[0].astype(BF16)

    s_row = lax.broadcasted_iota(jnp.int32, (TR, 128), 0)

    def contract(ref, masked):
        def step(pair, carry):
            cols = []
            for j in range(2):
                t = pair * 2 + j
                blocks = [ref[p, t, :, pl.ds(c * 128, 128)] for p in range(2) for c in range(8)]
                if masked:
                    keep = s_row <= h * TP + t - r * TR
                    blocks = [jnp.where(keep, b, jnp.zeros((), BF16)) for b in blocks]
                cols.append(jnp.concatenate(blocks, axis=0))
            out = jnp.dot(lmat[...], jnp.concatenate(cols, axis=1), preferred_element_type=F32) * weight
            for j in range(2):
                for po in range(2):
                    def block(q, b):
                        first = po * 128 + q * 32 + b * 8
                        return out[first : first + 8, j * 128 : j * 128 + 128]

                    total = by_group([block(q, q) for q in range(4)])
                    for d in range(1, 4):
                        moved = by_group([block(q, (q + d) % 4) for q in range(4)])
                        total = total + pltpu.roll(moved, 32 * d, 1)
                    at = (pair * 2 + j) * 2 + po
                    if masked:
                        fpart[at] += total
                    else:
                        fpart[at] = total
            return carry

        lax.fori_loop(0, TP // 2, step, 0)

    les_load.wait()
    for d in range(1, NX):
        arrived(sig_own.at[0], sx_recv + d - 1)
    left_matrix(0)
    contract(lesv, False)
    adv_load.wait()

    @pl.when(late)
    def _():
        for d in range(1, NX):
            arrived(sig_own.at[1], sx_recv + 3 + d - 1)
        left_matrix(1)
        contract(advv, True)

    rs_send, rs_recv = slots("send", 7), slots("recv", 7)
    for d in range(1, NR):
        start(None, fpart.at[pl.ds(3 * ((r + d) % NR), 3)], rs_buf.at[d - 1], rs_send + d - 1, rs_recv + d - 1, at_r(d))

    cz_send, cz_recv = slots("send", 7), slots("recv", 7)

    @pl.when(early)
    def _():
        for d in range(1, NX):
            arrived(col_x.at[d - 1], cx_recv + d - 1)
        total = col_send[x].astype(F32)
        for d in range(1, NX):
            total = total + col_x[d - 1].astype(F32)
        for j in range(OWNERS):
            colz_send[j] = total[j * 32 : j * 32 + 32]

    for d in range(1, NZ):
        to = (z + d) % NZ
        start(
            early & (to < OWNERS), colz_send.at[lax.rem(to, OWNERS)], col_z.at[d - 1], cz_send + d - 1, cz_recv + d - 1, at_z(d)
        )

    for d in range(1, NZ):
        arrived(tot_z.at[0], tz_recv + d - 1)
    above = jnp.zeros((8, 128), F32)
    for j in range(NZ):
        above = above + jnp.where(j > z, tot_z[j], 0.0)
    for j in range(NX):
        above = above + jnp.where(j > x, tot_x[j], 0.0)
    row_i = lax.broadcasted_iota(jnp.int32, (TP, TP), 0)
    later = jnp.where(lax.broadcasted_iota(jnp.int32, (TP, TP), 1) >= row_i, 1.0, 0.0)
    summed = jnp.dot(later, logs, precision=HIGHEST, preferred_element_type=F32) + above[0:1, 0:64]
    magnitude = jnp.exp(summed[:, 0:32])
    angle = summed[:, 32:64]
    factor = jnp.concatenate([magnitude * jnp.cos(angle), -magnitude * jnp.sin(angle)], axis=0)
    spread = jnp.where(
        lax.broadcasted_iota(jnp.int32, (32, 1024), 1) // 32 == lax.broadcasted_iota(jnp.int32, (32, 1024), 0), 1.0, 0.0
    )
    spread = jnp.dot(factor, spread, precision=HIGHEST, preferred_element_type=F32)
    for c in range(8):
        facv[pl.ds(c, 2 * TP, stride=8), :] = spread[:, c * 128 : c * 128 + 128]

    ag_send, ag_recv = slots("send", 7), slots("recv", 7)
    own = fpart[pl.ds(3 * r, 3)]
    for d in range(1, NR):
        arrived(rs_buf.at[d - 1], rs_recv + d - 1)
        own = own + rs_buf[d - 1]
    ag_buf[pl.ds(3 * r, 3)] = own
    for d in range(1, NR):
        start(None, ag_buf.at[pl.ds(3 * r, 3)], ag_buf.at[pl.ds(3 * r, 3)], ag_send + d - 1, ag_recv + d - 1, at_r(d))

    cg_send, cg_recv = slots("send", 7), slots("recv", 7)
    owner = z < OWNERS

    @pl.when(owner)
    def _():
        @pl.when(early)
        def _():
            col_own[...] = colz_send[lax.rem(z, OWNERS)]

        @pl.when(jnp.logical_not(early))
        def _():
            col_own[...] = jnp.zeros_like(col_own)

        for d in range(1, NZ):
            @pl.when((z - d + NZ) % NZ <= r)
            def _():
                arrived(col_z.at[d - 1], cz_recv + d - 1)
                col_own[...] += col_z[d - 1]

        col_all[x, lax.rem(z, OWNERS)] = col_own[...].astype(BF16)

    piece = col_all.at[x, lax.rem(z, OWNERS)]
    for d in range(1, NZ):
        start(owner, piece, piece, cg_send + d - 1, cg_recv + d - 1, at_z(d))

    for d in range(1, NR):
        arrived(rs_buf.at[0], ag_recv + d - 1)
    squares = jnp.zeros((8, 128), F32)
    for t in range(TP):
        fr, fi = facv[pl.ds(t * 8, 8), :], facv[pl.ds((TP + t) * 8, 8), :]
        ar = xv[pl.ds(t * 16, 8, stride=2), :] + ag_buf[2 * t]
        ai = xv[pl.ds(t * 16 + 1, 8, stride=2), :] + ag_buf[2 * t + 1]
        step_r, step_i = fr * ar - fi * ai, fr * ai + fi * ar
        stepv[2 * t] = step_r
        stepv[2 * t + 1] = step_i
        squares = squares + (step_r * step_r + step_i * step_i)
    nrm_x[x] = squares
    nx_send, nx_recv = slots("send", 3), slots("recv", 3)
    for d in range(1, NX):
        start(None, nrm_x.at[x], nrm_x.at[x], nx_send + d - 1, nx_recv + d - 1, at_x(d))

    ca_send, ca_recv = slots("send", 3), slots("recv", 3)
    for d in range(1, NZ):
        @pl.when((z - d + NZ) % NZ < OWNERS)
        def _():
            arrived(col_all.at[0, 0], cg_recv + d - 1)
    for d in range(1, NX):
        start(None, col_all.at[x], col_all.at[x], ca_send + d - 1, ca_recv + d - 1, at_x(d))

    nz_send, nz_recv = slots("send", 7), slots("recv", 7)
    for d in range(1, NX):
        arrived(nrm_x.at[0], nx_recv + d - 1)
    nrm_z[z] = nrm_x[0] + nrm_x[1] + nrm_x[2] + nrm_x[3]
    for d in range(1, NZ):
        start(None, nrm_z.at[z], nrm_z.at[z], nz_send + d - 1, nz_recv + d - 1, at_z(d))
    for d in range(1, NZ):
        arrived(nrm_z.at[0], nz_recv + d - 1)
    total = nrm_z[0]
    for j in range(1, NZ):
        total = total + nrm_z[j]
    total = jnp.sum(jnp.sum(total, axis=0, keepdims=True), axis=1, keepdims=True)
    scale = 1.0 / jnp.sqrt(total / float(2 * NX * NZ * TP * 1024) + 1e-6)
    for t in range(TP):
        out_ref[pl.ds(t * 16, 8, stride=2), :] = stepv[2 * t] * scale
        out_ref[pl.ds(t * 16 + 1, 8, stride=2), :] = stepv[2 * t + 1] * scale

    for d in range(1, NX):
        arrived(col_all.at[0], ca_recv + d - 1)
    col_ref[...] = col_all[...]

    for cond, args in pending:
        if cond is None:
            copy(*args).wait_send()
        else:
            @pl.when(cond)
            def _():
                copy(*args).wait_send()
    assert counts["send"] <= SENDS and counts["recv"] <= RECVS, counts


SENDS = 80
RECVS = 64


def shards(row_less, row_great, coupling, damping, phases, lesser_hist, advanced_hist, retarded_hist):
    def rows(a):
        a = a.transpose(1, 0, 2).reshape(TP, 2, 8, 128)
        return a.transpose(0, 2, 1, 3).reshape(TP * 16, 128)

    one, two, three = (jnp.asarray(m, BF16) for m in lane_order())
    anywhere = pl.BlockSpec(memory_space=pl.ANY)
    vmem = pl.BlockSpec(memory_space=pltpu.VMEM)
    scratch = [
        pltpu.VMEM((TP * 16, 128), F32),
        pltpu.VMEM((TP * 16, 128), F32),
        pltpu.VMEM((32, 32), F32),
        pltpu.VMEM((TP, 32), F32),
        pltpu.VMEM((TP, 32), F32),
        pltpu.VMEM((2, TP, TR, 1024), BF16),
        pltpu.VMEM((2, TP, TR, 1024), BF16),
        pltpu.VMEM((2, TP, TR, 1024), BF16),
        pltpu.VMEM((TP * 32, 512), BF16),
        pltpu.VMEM((NX * 128, 8 * TR), BF16),
        pltpu.VMEM((128, 128), BF16),
        pltpu.VMEM((2, 64, TP * 32), BF16),
        pltpu.VMEM((2, NX, 64, TP * 32), BF16),
        pltpu.VMEM((TP, 256, 256), BF16),
        pltpu.VMEM((8 * TR, 256), F32),
        pltpu.VMEM((NX, 4 * TR, 128), BF16),
        pltpu.VMEM((NX - 1, 4 * TR, 128), BF16),
        pltpu.VMEM((OWNERS, 32, 128), F32),
        pltpu.VMEM((NZ - 1, 32, 128), F32),
        pltpu.VMEM((32, 128), F32),
        pltpu.VMEM((NX, OWNERS, 32, 128), BF16),
        pltpu.VMEM((256, 768), BF16),
        pltpu.VMEM((2 * TP, 8, 128), F32),
        pltpu.VMEM((NR - 1, 3, 8, 128), F32),
        pltpu.VMEM((2 * TP, 8, 128), F32),
        pltpu.VMEM((NX, 8, 128), F32),
        pltpu.VMEM((NZ, 8, 128), F32),
        pltpu.VMEM((NX, 8, 128), F32),
        pltpu.VMEM((NZ, 8, 128), F32),
        pltpu.VMEM((2 * TP * 8, 128), F32),
        pltpu.VMEM((2 * TP, 8, 128), F32),
        pltpu.SemaphoreType.DMA((11,)),
        pltpu.SemaphoreType.DMA((SENDS,)),
        pltpu.SemaphoreType.DMA((RECVS,)),
    ]
    stepped, column = pl.pallas_call(
        body,
        out_shape=(
            jax.ShapeDtypeStruct((TP * 16, 128), F32),
            jax.ShapeDtypeStruct((NX, OWNERS, 32, 128), BF16),
        ),
        in_specs=[anywhere] * 11,
        out_specs=(vmem, vmem),
        scratch_shapes=scratch,
        compiler_params=pltpu.CompilerParams(
            collective_id=0, has_side_effects=True, vmem_limit_bytes=48 * 1024 * 1024
        ),
        name="kadanoff_baym_step",
    )(
        rows(row_less), rows(row_great), coupling, damping, phases,
        lesser_hist.transpose(0, 2, 1, 3), advanced_hist.transpose(0, 2, 1, 3), retarded_hist.transpose(0, 2, 1, 3),
        one, two, three,
    )
    stepped = stepped.reshape(TP, 8, 2, 128).transpose(2, 0, 1, 3).reshape(2, TP, 1024)
    column = column.reshape(NX, 2, 2, TR, 128).transpose(2, 3, 0, 1, 4).reshape(2, TR, 1024)
    return stepped, column.astype(F32)


def solution(mesh):
    return jax.shard_map(
        shards,
        mesh=mesh,
        in_specs=(
            P(None, "hist", None),
            P(None, "hist", None),
            P(),
            P("hist", None),
            P("hist", None),
            P(None, "row", "hist", None),
            P(None, "row", "hist", None),
            P(None, "row", "hist", None),
        ),
        out_specs=(P(None, "hist", None), P(None, "row", None)),
        check_vma=False,
    )
```

```python
import functools

import jax
import jax.numpy as jnp
import numpy as np
from jax import lax
from jax.experimental import pallas as pl
from jax.experimental.pallas import tpu as pltpu
from jax.sharding import PartitionSpec as P

MESH = pl.DeviceIdType.MESH
F32 = jnp.float32
BF16 = jnp.bfloat16
HIGHEST = lax.Precision.HIGHEST
NX = 4
NZ = 8
NY = 4
NH = NX * NZ
TP = 12
TR = 48
OWNERS = 6
LANES_TO_LANES = (((1,), (1,)), ((), ()))


def lane_order():
    one = np.zeros((TP * 32, 4 * 128), np.float32)
    two = np.zeros((NX * 128, 8 * TR), np.float32)
    for s in range(TP):
        for c in range(8):
            for q in range(4):
                one[s * 32 + 4 * c + q, q * 128 + c * TP + s] = 1
            for x in range(NX):
                two[x * 128 + c * TP + s, c * TR + x * TP + s] = 1
    three = np.zeros((128, 128), np.float32)
    for q in range(4):
        for a in range(4):
            for c in range(8):
                three[q * 32 + a * 8 + c, q * 32 + 4 * c + a] = 1
    return one, two, three


def body(
    x_hbm, y_hbm, c_hbm, damp_hbm, phase_hbm, les_hbm, adv_hbm, ret_hbm, one_hbm, two_hbm, three_hbm,
    out_ref, col_ref,
    xv, yv, cv, dampv, phasev, lesv, advv, retv, onev, twov, threev,
    sig_own, sig_all, bmat, col_acc, col_send, col_x, colz_send, col_z, col_own, col_all,
    lmat, fpart, rs_buf, y_buf, ag_buf, tot_x, tot_z, norms, facv, stepv,
    load_sem, send_sem, recv_sem,
):
    h = lax.axis_index("hist")
    r = lax.axis_index("row")
    z, x = h // NX, h % NX
    y, core = r // 2, r % 2
    dz = (z - r + NZ) % NZ
    early = z <= r
    late = z >= r

    def at_x(d):
        return {"hist": z * NX + (x + d) % NX}

    def at_z(d):
        return {"hist": ((z + d + NZ) % NZ) * NX + x}

    def at_h(d):
        return {"hist": (h + d) % NH}

    def at_core():
        return {"row": 2 * y + 1 - core}

    def at_y(d):
        return {"row": 2 * ((y + d) % NY) + core}

    counts = {"send": 0, "recv": 0}
    pending = []

    def slots(kind, n):
        first = counts[kind]
        counts[kind] += n
        return first

    def copy(src, dst, send, recv, device):
        return pltpu.make_async_remote_copy(
            src_ref=src, dst_ref=dst, send_sem=send_sem.at[send], recv_sem=recv_sem.at[recv],
            device_id=device, device_id_type=MESH,
        )

    def start(cond, *args):
        if cond is None:
            copy(*args).start()
        else:
            @pl.when(cond)
            def _():
                copy(*args).start()
        pending.append((cond, args))

    def arrived(ref, recv):
        copy(ref, ref, 0, recv, at_x(1)).wait_recv()

    loads = []
    for src, dst in (
        (c_hbm, cv), (x_hbm, xv), (y_hbm, yv), (damp_hbm, dampv), (phase_hbm, phasev),
        (one_hbm, onev), (two_hbm, twov), (three_hbm, threev), (ret_hbm, retv), (les_hbm, lesv), (adv_hbm, advv),
    ):
        loads.append(pltpu.make_async_copy(src, dst, load_sem.at[len(loads)]))
        loads[-1].start()
    (c_load, x_load, y_load, damp_load, phase_load, one_load, two_load, three_load, ret_load, les_load, adv_load) = loads

    barrier = pltpu.get_barrier_semaphore()
    for d in range(1, NH):
        pl.semaphore_signal(barrier, inc=1, device_id=at_h(d), device_id_type=MESH)
    for device in [at_core()] + [at_y(d) for d in range(1, NY)]:
        pl.semaphore_signal(barrier, inc=1, device_id=device, device_id_type=MESH)

    lane8 = lax.broadcasted_iota(jnp.int32, (8, 128), 1) // 32

    def by_group(parts):
        mask = lane8.reshape((1,) * (parts[0].ndim - 2) + (8, 128))
        out = parts[0]
        for g in range(1, 4):
            out = jnp.where(mask == g, parts[g], out)
        return out

    def rolled(a):
        flat = a.reshape(-1, 128)
        return [a] + [pltpu.roll(flat, 32 * d, 1).reshape(a.shape) for d in range(1, 4)]

    c_load.wait()
    coup = cv[...]
    wide = jnp.concatenate([coup] * 4, axis=1)
    square = jnp.concatenate([wide] * 4, axis=0)
    same = (
        lax.broadcasted_iota(jnp.int32, (128, 128), 0) // 32
        == lax.broadcasted_iota(jnp.int32, (128, 128), 1) // 32
    )
    right = jnp.where(same, square, 0.0)
    rows4 = [cv[pl.ds(g, 8, stride=4), :] for g in range(4)]
    col_of = [[jnp.broadcast_to(rows4[g][:, k : k + 1], (8, 128)) for k in range(32)] for g in range(4)]

    x_load.wait()
    y_load.wait()

    def part(ref, p):
        return ref[pl.ds(p, TP * 8, stride=2), :]

    xr, xi, yr, yi = part(xv, 0), part(xv, 1), part(yv, 0), part(yv, 1)
    polar = jnp.concatenate([-(xr * yr + xi * yi), -(xi * yr - xr * yi)], axis=0)
    half = lax.dot_general(polar, right, LANES_TO_LANES, precision=HIGHEST, preferred_element_type=F32)
    half = half.reshape(2 * TP, 8, 128)
    half_d = rolled(half)
    screen = jnp.zeros((2 * TP, 8, 128), F32)
    for d in range(4):
        for c in range(8):
            factor = by_group([col_of[g][4 * c + (g - d) % 4] for g in range(4)])
            screen = screen + factor[None] * half_d[d][:, c : c + 1, :]
    sr, si = screen[:TP], screen[TP:]
    xr, xi, yr, yi = (a.reshape(TP, 8, 128) for a in (xr, xi, yr, yi))
    less = (xr * sr - xi * si, xr * si + xi * sr)
    great = (yr * sr + yi * si, yi * sr - yr * si)
    ret = (great[0] - less[0], great[1] - less[1])
    less_d = [rolled(a) for a in less]
    for a, pair in enumerate(([rolled(v) for v in ret], less_d)):
        for p in range(2):
            for m in range(3):
                block = jnp.concatenate(
                    [by_group([pair[p][(g - b) % 4][4 * m + g] for g in range(4)]) for b in range(4)], axis=0
                )
                sig_own[a, pl.ds(p * 32, 32), pl.ds(m * 128, 128)] = block.astype(BF16)

    damp_load.wait()
    phase_load.wait()
    logs = jnp.concatenate([jnp.log(dampv[...]), phasev[...]], axis=1)
    tot = jnp.sum(logs, axis=0, keepdims=True)
    tot = jnp.concatenate([tot, jnp.zeros((1, 64), F32)], axis=1)
    tot_x[x] = jnp.broadcast_to(tot, (8, 128))

    pl.semaphore_wait(barrier, (NH - 1) + 1 + (NY - 1))

    source = z == r
    z_send, z_recv = slots("send", 14), slots("recv", 2)
    for a in range(2):
        for d in (4, 3, 5, 2, 6, 1, 7):
            cond = source if a == 0 else source & ((z + d) % NZ > r)
            start(cond, sig_own.at[a], sig_all.at[a, x], z_send + 7 * a + d - 1, z_recv + a, at_z(d))

    @pl.when(source)
    def _():
        sig_all[:, x] = sig_own[...]

    sx_send, sx_recv = slots("send", 6), slots("recv", 6)

    def round_x(a, cond):
        for d in range(1, NX):
            start(
                cond, sig_all.at[a, x], sig_all.at[a, x], sx_send + 3 * a + d - 1, sx_recv + 3 * a + d - 1, at_x(d)
            )

    for a in range(2):
        round_x(a, source)

    tx_send, tx_recv = slots("send", 3), slots("recv", 3)
    for d in range(1, NX):
        start(None, tot_x.at[x], tot_x.at[x], tx_send + d - 1, tx_recv + d - 1, at_x(d))

    @pl.when(early)
    def _():
        def square_of(p, s):
            rows = []
            for g in range(4):
                for b in range(4):
                    rows.append(jnp.where(lane8 == g, less_d[p][(g - b) % 4][s], 0.0))
            return jnp.concatenate(rows, axis=0)

        for s in range(TP):
            b0, b1 = square_of(0, s), square_of(1, s)
            bmat[s, pl.ds(0, 128), pl.ds(0, 128)] = b0.astype(BF16)
            bmat[s, pl.ds(0, 128), pl.ds(128, 128)] = b1.astype(BF16)
            bmat[s, pl.ds(128, 128), pl.ds(0, 128)] = (-b1).astype(BF16)
            bmat[s, pl.ds(128, 128), pl.ds(128, 128)] = b0.astype(BF16)

    weight = float(NX * NZ * TP * 32) ** -0.5
    ret_load.wait()
    three_load.wait()
    cx_send, cx_recv = slots("send", 3), slots("recv", 3)

    @pl.when(early)
    def _():
        t_row = lax.broadcasted_iota(jnp.int32, (TR, 128), 0)
        col_acc[...] = jnp.zeros_like(col_acc)

        def step(s, carry):
            keep = t_row >= h * TP + s - r * TR
            rows = [
                jnp.concatenate(
                    [jnp.where(keep, retv[p, s, :, pl.ds(c * 128, 128)], jnp.zeros((), BF16)) for p in range(2)], axis=1
                )
                for c in range(8)
            ]
            col_acc[...] += lax.dot_general(
                jnp.concatenate(rows, axis=0), bmat[s], LANES_TO_LANES, preferred_element_type=F32
            )
            return carry

        lax.fori_loop(0, TP, step, 0)
        for c in range(8):
            for po in range(2):
                value = (col_acc[pl.ds(c * TR, TR), pl.ds(po * 128, 128)] * -weight).astype(BF16)
                value = jnp.dot(value, threev[...], preferred_element_type=F32)
                col_send[c // 2, pl.ds(((c % 2) * 2 + po) * TR, TR), :] = value.astype(BF16)

    for d in range(1, NX):
        start(early, col_send.at[(x + d) % NX], col_x.at[d - 1], cx_send + d - 1, cx_recv + d - 1, at_x(d))

    for a, cond in enumerate((jnp.logical_not(source), z > r)):
        @pl.when(cond)
        def _():
            arrived(sig_own.at[a], z_recv + a)

        round_x(a, cond)

    tz_send, tz_recv = slots("send", 7), slots("recv", 7)
    for d in range(1, NX):
        arrived(tot_x.at[0], tx_recv + d - 1)
    tot_z[z] = tot_x[0] + tot_x[1] + tot_x[2] + tot_x[3]
    for d in range(1, NZ):
        start(None, tot_z.at[z], tot_z.at[z], tz_send + d - 1, tz_recv + d - 1, at_z(d))

    cz_send, cz_recv = slots("send", 7), slots("recv", 7)

    @pl.when(early)
    def _():
        for d in range(1, NX):
            arrived(col_x.at[d - 1], cx_recv + d - 1)
        total = col_send[x].astype(F32)
        for d in range(1, NX):
            total = total + col_x[d - 1].astype(F32)
        for j in range(OWNERS):
            colz_send[j] = total[j * 32 : j * 32 + 32]

    for d in range(1, NZ):
        to = (z + d) % NZ
        start(
            early & (to < OWNERS), colz_send.at[lax.rem(to, OWNERS)], col_z.at[d - 1], cz_send + d - 1, cz_recv + d - 1, at_z(d)
        )

    one_load.wait()
    two_load.wait()

    def left_matrix(a):
        blocks = [
            jnp.dot(sig_all[a, j], onev[...], preferred_element_type=F32).astype(BF16) for j in range(NX)
        ]
        parts = []
        for p in range(2):
            gathered = jnp.concatenate(
                [
                    jnp.concatenate([b[p * 32 : p * 32 + 32, q * 128 : q * 128 + 128] for b in blocks], axis=1)
                    for q in range(4)
                ],
                axis=0,
            )
            parts.append(jnp.dot(gathered, twov[...], preferred_element_type=F32))
        lmat[pl.ds(0, 128), pl.ds(0, 384)] = parts[0].astype(BF16)
        lmat[pl.ds(0, 128), pl.ds(384, 384)] = (-parts[1]).astype(BF16)
        lmat[pl.ds(128, 128), pl.ds(0, 384)] = parts[1].astype(BF16)
        lmat[pl.ds(128, 128), pl.ds(384, 384)] = parts[0].astype(BF16)

    s_row = lax.broadcasted_iota(jnp.int32, (TR, 128), 0)

    def contract(ref, masked, half):
        def step(index, carry):
            pair = half * 3 + index
            cols = []
            for j in range(2):
                t = pair * 2 + j
                blocks = [ref[p, t, :, pl.ds(c * 128, 128)] for p in range(2) for c in range(8)]
                if masked:
                    keep = s_row <= h * TP + t - r * TR
                    blocks = [jnp.where(keep, b, jnp.zeros((), BF16)) for b in blocks]
                cols.append(jnp.concatenate(blocks, axis=0))
            out = jnp.dot(lmat[...], jnp.concatenate(cols, axis=1), preferred_element_type=F32) * weight
            for j in range(2):
                for po in range(2):
                    def block(q, b):
                        first = po * 128 + q * 32 + b * 8
                        return out[first : first + 8, j * 128 : j * 128 + 128]

                    total = by_group([block(q, q) for q in range(4)])
                    for d in range(1, 4):
                        moved = by_group([block(q, (q + d) % 4) for q in range(4)])
                        total = total + pltpu.roll(moved, 32 * d, 1)
                    at = (pair * 2 + j) * 2 + po
                    if masked:
                        fpart[at] += total
                    else:
                        fpart[at] = total
            return carry

        lax.fori_loop(0, TP // 4, step, 0)

    les_load.wait()
    for d in range(1, NX):
        arrived(sig_own.at[0], sx_recv + d - 1)
    left_matrix(0)
    contract(lesv, False, 1 - core)
    contract(lesv, False, core)
    adv_load.wait()

    @pl.when(late)
    def _():
        for d in range(1, NX):
            arrived(sig_own.at[1], sx_recv + 3 + d - 1)
        left_matrix(1)
        contract(advv, True, 1 - core)

    rc_send, rc_recv = slots("send", 1), slots("recv", 1)
    start(None, fpart.at[pl.ds(TP * (1 - core), TP)], rs_buf, rc_send, rc_recv, at_core())

    @pl.when(late)
    def _():
        contract(advv, True, core)

    arrived(rs_buf, rc_recv)
    ry_send, ry_recv = slots("send", 3), slots("recv", 3)
    half = fpart[pl.ds(TP * core, TP)] + rs_buf[...]
    y_buf[y] = half.reshape(TP * 8, 128).astype(BF16)
    for d in range(1, NY):
        start(None, y_buf.at[y], y_buf.at[y], ry_send + d - 1, ry_recv + d - 1, at_y(d))

    cg_send, cg_recv = slots("send", 7), slots("recv", 7)
    owner = z < OWNERS

    @pl.when(owner)
    def _():
        @pl.when(early)
        def _():
            col_own[...] = colz_send[lax.rem(z, OWNERS)]

        @pl.when(jnp.logical_not(early))
        def _():
            col_own[...] = jnp.zeros_like(col_own)

        for d in range(1, NZ):
            @pl.when((z - d + NZ) % NZ <= r)
            def _():
                arrived(col_z.at[d - 1], cz_recv + d - 1)
                col_own[...] += col_z[d - 1]

        col_all[x, lax.rem(z, OWNERS)] = col_own[...].astype(BF16)

    piece = col_all.at[x, lax.rem(z, OWNERS)]
    for d in range(1, NZ):
        start(owner, piece, piece, cg_send + d - 1, cg_recv + d - 1, at_z(d))

    for d in range(1, NZ):
        arrived(tot_z.at[0], tz_recv + d - 1)
    above = jnp.zeros((8, 128), F32)
    for j in range(NZ):
        above = above + jnp.where(j > z, tot_z[j], 0.0)
    for j in range(NX):
        above = above + jnp.where(j > x, tot_x[j], 0.0)
    row_i = lax.broadcasted_iota(jnp.int32, (TP, TP), 0)
    later = jnp.where(lax.broadcasted_iota(jnp.int32, (TP, TP), 1) >= row_i, 1.0, 0.0)
    summed = jnp.dot(later, logs, precision=HIGHEST, preferred_element_type=F32) + above[0:1, 0:64]
    magnitude = jnp.exp(summed[:, 0:32])
    angle = summed[:, 32:64]
    factor = jnp.concatenate([magnitude * jnp.cos(angle), -magnitude * jnp.sin(angle)], axis=0)
    spread = jnp.where(
        lax.broadcasted_iota(jnp.int32, (32, 1024), 1) // 32 == lax.broadcasted_iota(jnp.int32, (32, 1024), 0), 1.0, 0.0
    )
    spread = jnp.dot(factor, spread, precision=HIGHEST, preferred_element_type=F32)
    for c in range(8):
        facv[pl.ds(c, 2 * TP, stride=8), :] = spread[:, c * 128 : c * 128 + 128]

    ra_send, ra_recv = slots("send", 1), slots("recv", 1)
    for d in range(1, NY):
        arrived(y_buf.at[0], ry_recv + d - 1)
    half = y_buf[0].astype(F32)
    for j in range(1, NY):
        half = half + y_buf[j].astype(F32)
    ag_buf[pl.ds(TP * core, TP)] = half.reshape(TP, 8, 128)
    piece = ag_buf.at[pl.ds(TP * core, TP)]
    start(None, piece, piece, ra_send, ra_recv, at_core())

    arrived(rs_buf, ra_recv)
    squares = jnp.zeros((8, 128), F32)
    for t in range(TP):
        fr, fi = facv[pl.ds(t * 8, 8), :], facv[pl.ds((TP + t) * 8, 8), :]
        ar = xv[pl.ds(t * 16, 8, stride=2), :] + ag_buf[2 * t]
        ai = xv[pl.ds(t * 16 + 1, 8, stride=2), :] + ag_buf[2 * t + 1]
        step_r, step_i = fr * ar - fi * ai, fr * ai + fi * ar
        stepv[2 * t] = step_r
        stepv[2 * t + 1] = step_i
        squares = squares + (step_r * step_r + step_i * step_i)
    norms[h] = jnp.sum(squares, axis=0, keepdims=True)
    n_send, n_recv = slots("send", NH - 1), slots("recv", NH - 1)
    for d in range(1, NH):
        start(None, norms.at[h], norms.at[h], n_send + d - 1, n_recv + d - 1, at_h(d))

    ca_send, ca_recv = slots("send", 3), slots("recv", 3)
    for d in range(1, NZ):
        @pl.when((z - d + NZ) % NZ < OWNERS)
        def _():
            arrived(col_all.at[0, 0], cg_recv + d - 1)
    for d in range(1, NX):
        start(None, col_all.at[x], col_all.at[x], ca_send + d - 1, ca_recv + d - 1, at_x(d))

    for d in range(1, NH):
        arrived(norms.at[0], n_recv + d - 1)
    total = jnp.sum(norms[...], axis=0)
    total = jnp.sum(total, axis=1, keepdims=True)
    scale = 1.0 / jnp.sqrt(total / float(2 * NX * NZ * TP * 1024) + 1e-6)
    for t in range(TP):
        out_ref[pl.ds(t * 16, 8, stride=2), :] = stepv[2 * t] * scale
        out_ref[pl.ds(t * 16 + 1, 8, stride=2), :] = stepv[2 * t + 1] * scale

    for d in range(1, NX):
        arrived(col_all.at[0], ca_recv + d - 1)
    for j in range(NX):
        rows = col_all[j].reshape(4 * TR, 128)
        for c in range(2):
            for po in range(2):
                first = (2 * c + po) * TR
                col_ref[po, :, pl.ds((2 * j + c) * 128, 128)] = rows[first : first + TR]

    for cond, args in pending:
        if cond is None:
            copy(*args).wait_send()
        else:
            @pl.when(cond)
            def _():
                copy(*args).wait_send()
    assert counts["send"] <= SENDS and counts["recv"] <= RECVS, counts


SENDS = 112
RECVS = 96


def shards(row_less, row_great, coupling, damping, phases, lesser_hist, advanced_hist, retarded_hist):
    def rows(a):
        a = a.transpose(1, 0, 2).reshape(TP, 2, 8, 128)
        return a.transpose(0, 2, 1, 3).reshape(TP * 16, 128)

    one, two, three = (jnp.asarray(m, BF16) for m in lane_order())
    anywhere = pl.BlockSpec(memory_space=pltpu.HBM)
    vmem = pl.BlockSpec(memory_space=pltpu.VMEM)
    scratch = [
        pltpu.VMEM((TP * 16, 128), F32),
        pltpu.VMEM((TP * 16, 128), F32),
        pltpu.VMEM((32, 32), F32),
        pltpu.VMEM((TP, 32), F32),
        pltpu.VMEM((TP, 32), F32),
        pltpu.VMEM((2, TP, TR, 1024), BF16),
        pltpu.VMEM((2, TP, TR, 1024), BF16),
        pltpu.VMEM((2, TP, TR, 1024), BF16),
        pltpu.VMEM((TP * 32, 512), BF16),
        pltpu.VMEM((NX * 128, 8 * TR), BF16),
        pltpu.VMEM((128, 128), BF16),
        pltpu.VMEM((2, 64, TP * 32), BF16),
        pltpu.VMEM((2, NX, 64, TP * 32), BF16),
        pltpu.VMEM((TP, 256, 256), BF16),
        pltpu.VMEM((8 * TR, 256), F32),
        pltpu.VMEM((NX, 4 * TR, 128), BF16),
        pltpu.VMEM((NX - 1, 4 * TR, 128), BF16),
        pltpu.VMEM((OWNERS, 32, 128), F32),
        pltpu.VMEM((NZ - 1, 32, 128), F32),
        pltpu.VMEM((32, 128), F32),
        pltpu.VMEM((NX, OWNERS, 32, 128), BF16),
        pltpu.VMEM((256, 768), BF16),
        pltpu.VMEM((2 * TP, 8, 128), F32),
        pltpu.VMEM((TP, 8, 128), F32),
        pltpu.VMEM((NY, TP * 8, 128), BF16),
        pltpu.VMEM((2 * TP, 8, 128), F32),
        pltpu.VMEM((NX, 8, 128), F32),
        pltpu.VMEM((NZ, 8, 128), F32),
        pltpu.VMEM((NH, 1, 128), F32),
        pltpu.VMEM((2 * TP * 8, 128), F32),
        pltpu.VMEM((2 * TP, 8, 128), F32),
        pltpu.SemaphoreType.DMA((11,)),
        pltpu.SemaphoreType.DMA((SENDS,)),
        pltpu.SemaphoreType.DMA((RECVS,)),
    ]
    operands = (
        rows(row_less), rows(row_great), coupling, damping, phases,
        lesser_hist.transpose(0, 2, 1, 3), advanced_hist.transpose(0, 2, 1, 3), retarded_hist.transpose(0, 2, 1, 3),
        one, two, three,
    )
    stepped, column = pl.pallas_call(
        body,
        out_shape=(
            jax.ShapeDtypeStruct((TP * 16, 128), F32),
            jax.ShapeDtypeStruct((2, TR, 1024), BF16),
        ),
        in_specs=[anywhere] * 11,
        out_specs=(vmem, vmem),
        scratch_shapes=scratch,
        compiler_params=pltpu.CompilerParams(
            collective_id=0, has_side_effects=True, vmem_limit_bytes=24 * 1024 * 1024
        ),
        name="kadanoff_baym_step",
    )(
        *(pltpu.with_memory_space_constraint(a, pltpu.HBM) for a in operands)
    )
    stepped = stepped.reshape(TP, 8, 2, 128).transpose(2, 0, 1, 3).reshape(2, TP, 1024)
    return stepped, column.astype(F32)


def solution(mesh):
    return jax.shard_map(
        shards,
        mesh=mesh,
        in_specs=(
            P(None, "hist", None),
            P(None, "hist", None),
            P(),
            P("hist", None),
            P("hist", None),
            P(None, "row", "hist", None),
            P(None, "row", "hist", None),
            P(None, "row", "hist", None),
        ),
        out_specs=(P(None, "hist", None), P(None, "row", None)),
        check_vma=False,
    )
```

```python
import functools

import jax
import jax.numpy as jnp
import numpy as np
from jax import lax
from jax.experimental import pallas as pl
from jax.experimental.pallas import tpu as pltpu
from jax.sharding import PartitionSpec as P

MESH = pl.DeviceIdType.MESH
F32 = jnp.float32
BF16 = jnp.bfloat16
HIGHEST = lax.Precision.HIGHEST
NX = 4
NZ = 8
NR = 8
NH = NX * NZ


def ring(n, d):
    return min(d, n - d)


SPREAD = {0: 4, 1: 3, 2: 5, 3: 2, 4: 7, 5: 0, 6: 6, 7: 1}
FAR_X = sorted(range(1, NX), key=lambda d: -ring(NX, d))
FAR_Z = sorted(range(1, NZ), key=lambda d: -ring(NZ, d))
FAR_R = sorted(range(1, NR), key=lambda d: -ring(NR, d))
FAR_H = sorted(
    ((dz, dx) for dz in range(NZ) for dx in range(NX) if dz or dx), key=lambda d: -ring(NZ, d[0]) - ring(NX, d[1])
)
TP = 12
TR = 48
OWNERS = 6
LANES_TO_LANES = (((1,), (1,)), ((), ()))


def lane_order():
    one = np.zeros((TP * 32, 4 * 128), np.float32)
    two = np.zeros((NX * 128, 8 * TR), np.float32)
    for s in range(TP):
        for c in range(8):
            for q in range(4):
                one[s * 32 + 4 * c + q, q * 128 + c * TP + s] = 1
            for x in range(NX):
                two[x * 128 + c * TP + s, c * TR + x * TP + s] = 1
    three = np.zeros((128, 128), np.float32)
    for q in range(4):
        for a in range(4):
            for c in range(8):
                three[q * 32 + a * 8 + c, q * 32 + 4 * c + a] = 1
    return one, two, three


def body(
    x_hbm, y_hbm, c_hbm, damp_hbm, phase_hbm, les_hbm, adv_hbm, ret_hbm, one_hbm, two_hbm, three_hbm,
    out_ref, col_ref,
    xv, yv, cv, dampv, phasev, lesv, advv, retv, onev, twov, threev,
    sig_own, sig_all, bmat, col_acc, col_send, col_x, colz_send, col_z, col_own, col_all,
    lmat, fpart, rs_buf, y_buf, tot_x, tot_z, norms, facv, stepv,
    load_sem, send_sem, recv_sem,
):
    h = lax.axis_index("hist")
    r = lax.axis_index("row")
    z, x = h // NX, h % NX
    y, core = r // 2, r % 2
    dz = (z - r + NZ) % NZ
    early = z <= r
    source = z == r
    place = (y - z // 2 + 4) % 4 * 2 + (core + z) % 2
    late = z >= r

    def at_x(d):
        return {"hist": z * NX + (x + d) % NX}

    def at_z(d):
        return {"hist": ((z + d + NZ) % NZ) * NX + x}

    def at_h(d):
        return {"hist": (z + d[0]) % NZ * NX + (x + d[1]) % NX}

    def at_core():
        return {"row": 2 * y + 1 - core}

    def at_r(d):
        return {"row": (r + d) % NR}

    counts = {"send": 0, "recv": 0}
    pending = []

    def slots(kind, n):
        first = counts[kind]
        counts[kind] += n
        return first

    def copy(src, dst, send, recv, device):
        return pltpu.make_async_remote_copy(
            src_ref=src, dst_ref=dst, send_sem=send_sem.at[send], recv_sem=recv_sem.at[recv],
            device_id=device, device_id_type=MESH,
        )

    def start(cond, *args):
        if cond is None:
            copy(*args).start()
        else:
            @pl.when(cond)
            def _():
                copy(*args).start()
        pending.append((cond, args))

    def arrived(ref, recv):
        copy(ref, ref, 0, recv, at_x(1)).wait_recv()

    loads = []
    for src, dst in (
        (c_hbm, cv), (x_hbm, xv), (y_hbm, yv), (damp_hbm, dampv), (phase_hbm, phasev),
        (one_hbm, onev), (two_hbm, twov), (three_hbm, threev), (ret_hbm, retv), (les_hbm, lesv), (adv_hbm, advv),
    ):
        loads.append(pltpu.make_async_copy(src, dst, load_sem.at[len(loads)]))
        loads[-1].start()
    (c_load, x_load, y_load, damp_load, phase_load, one_load, two_load, three_load, ret_load, les_load, adv_load) = loads

    barrier = pltpu.get_barrier_semaphore()
    for d in range(1, NX):
        pl.semaphore_signal(barrier, inc=1, device_id=at_x(d), device_id_type=MESH)
    for d in range(1, NZ):
        pl.semaphore_signal(barrier, inc=1, device_id=at_z(d), device_id_type=MESH)
    for device in [at_r(d) for d in range(1, NR)]:
        pl.semaphore_signal(barrier, inc=1, device_id=device, device_id_type=MESH)
    for k, d in SPREAD.items():
        @pl.when((z - r + NZ) % NZ == d)
        def _():
            holder = (r // 2 + k // 2) % 4 * 2 + (r + k) % 2
            pl.semaphore_signal(barrier, inc=1, device_id={"hist": r * NX + x, "row": holder}, device_id_type=MESH)

    lane8 = lax.broadcasted_iota(jnp.int32, (8, 128), 1) // 32

    def by_group(parts):
        mask = lane8.reshape((1,) * (parts[0].ndim - 2) + (8, 128))
        out = parts[0]
        for g in range(1, 4):
            out = jnp.where(mask == g, parts[g], out)
        return out

    def rolled(a):
        flat = a.reshape(-1, 128)
        return [a] + [pltpu.roll(flat, 32 * d, 1).reshape(a.shape) for d in range(1, 4)]

    c_load.wait()
    coup = cv[...]
    wide = jnp.concatenate([coup] * 4, axis=1)
    square = jnp.concatenate([wide] * 4, axis=0)
    same = (
        lax.broadcasted_iota(jnp.int32, (128, 128), 0) // 32
        == lax.broadcasted_iota(jnp.int32, (128, 128), 1) // 32
    )
    right = jnp.where(same, square, 0.0)
    rows4 = [cv[pl.ds(g, 8, stride=4), :] for g in range(4)]
    col_of = [[jnp.broadcast_to(rows4[g][:, k : k + 1], (8, 128)) for k in range(32)] for g in range(4)]

    x_load.wait()
    y_load.wait()

    def part(ref, p):
        return ref[pl.ds(p, TP * 8, stride=2), :]

    xr, xi, yr, yi = part(xv, 0), part(xv, 1), part(yv, 0), part(yv, 1)
    polar = jnp.concatenate([-(xr * yr + xi * yi), -(xi * yr - xr * yi)], axis=0)
    half = lax.dot_general(polar, right, LANES_TO_LANES, precision=HIGHEST, preferred_element_type=F32)
    half = half.reshape(2 * TP, 8, 128)
    half_d = rolled(half)
    screen = jnp.zeros((2 * TP, 8, 128), F32)
    for d in range(4):
        for c in range(8):
            factor = by_group([col_of[g][4 * c + (g - d) % 4] for g in range(4)])
            screen = screen + factor[None] * half_d[d][:, c : c + 1, :]
    sr, si = screen[:TP], screen[TP:]
    xr, xi, yr, yi = (a.reshape(TP, 8, 128) for a in (xr, xi, yr, yi))
    less = (xr * sr - xi * si, xr * si + xi * sr)
    great = (yr * sr + yi * si, yi * sr - yr * si)
    ret = (great[0] - less[0], great[1] - less[1])
    less_d = [rolled(a) for a in less]
    for a, pair in enumerate(([rolled(v) for v in ret], less_d)):
        for p in range(2):
            for m in range(3):
                block = jnp.concatenate(
                    [by_group([pair[p][(g - b) % 4][4 * m + g] for g in range(4)]) for b in range(4)], axis=0
                )
                sig_own[a, pl.ds(p * 32, 32), pl.ds(m * 128, 128)] = block.astype(BF16)

    damp_load.wait()
    phase_load.wait()
    logs = jnp.concatenate([jnp.log(dampv[...]), phasev[...]], axis=1)
    tot = jnp.sum(logs, axis=0, keepdims=True)
    tot = jnp.concatenate([tot, jnp.zeros((1, 64), F32)], axis=1)
    tot_x[x] = jnp.broadcast_to(tot, (8, 128))

    pl.semaphore_wait(barrier, (NX - 1) + (NZ - 1) + (NR - 1) + 1)

    z_send, z_recv = slots("send", 2), slots("recv", 2)
    for a in range(2):
        for k, d in SPREAD.items():
            if d == 0:
                continue
            start(
                (place == k) if a == 0 else (place == k) & ((z + d) % NZ > z),
                sig_own.at[a], sig_all.at[a, x], z_send + a, z_recv + a, {"hist": (z + d) % NZ * NX + x, "row": z},
            )

    @pl.when(source)
    def _():
        sig_all[:, x] = sig_own[...]

    sx_send, sx_recv = slots("send", 6), slots("recv", 6)

    def round_x(a, cond):
        for d in FAR_X:
            start(
                cond, sig_all.at[a, x], sig_all.at[a, x], sx_send + 3 * a + d - 1, sx_recv + 3 * a + d - 1, at_x(d)
            )

    for a in range(2):
        round_x(a, source)

    tx_send, tx_recv = slots("send", 3), slots("recv", 3)
    for d in FAR_X:
        start(None, tot_x.at[x], tot_x.at[x], tx_send + d - 1, tx_recv + d - 1, at_x(d))

    @pl.when(early)
    def _():
        def square_of(p, s):
            rows = []
            for g in range(4):
                for b in range(4):
                    rows.append(jnp.where(lane8 == g, less_d[p][(g - b) % 4][s], 0.0))
            return jnp.concatenate(rows, axis=0)

        for s in range(TP):
            b0, b1 = square_of(0, s), square_of(1, s)
            bmat[s // 4, pl.ds(0, 128), pl.ds(s % 4 * 256, 128)] = b0.astype(BF16)
            bmat[s // 4, pl.ds(0, 128), pl.ds(s % 4 * 256 + 128, 128)] = b1.astype(BF16)
            bmat[s // 4, pl.ds(128, 128), pl.ds(s % 4 * 256, 128)] = (-b1).astype(BF16)
            bmat[s // 4, pl.ds(128, 128), pl.ds(s % 4 * 256 + 128, 128)] = b0.astype(BF16)

    weight = float(NX * NZ * TP * 32) ** -0.5
    ret_load.wait()
    three_load.wait()
    cx_send, cx_recv = slots("send", 3), slots("recv", 3)

    @pl.when(early)
    def _():
        t_row = lax.broadcasted_iota(jnp.int32, (TR, 128), 0)
        col_acc[...] = jnp.zeros_like(col_acc)

        def step(group, carry):
            rows = []
            for c in range(8):
                lanes = []
                for k in range(4):
                    at = group * 4 + k
                    keep = t_row >= h * TP + at - r * TR
                    for p in range(2):
                        lanes.append(jnp.where(keep, retv[p, at, :, pl.ds(c * 128, 128)], jnp.zeros((), BF16)))
                rows.append(jnp.concatenate(lanes, axis=1))
            col_acc[...] += lax.dot_general(
                jnp.concatenate(rows, axis=0), bmat[group], LANES_TO_LANES, preferred_element_type=F32
            )
            return carry

        lax.fori_loop(0, TP // 4, step, 0)
        for c in range(8):
            for po in range(2):
                value = (col_acc[pl.ds(c * TR, TR), pl.ds(po * 128, 128)] * -weight).astype(BF16)
                value = jnp.dot(value, threev[...], preferred_element_type=F32)
                col_send[c // 2, pl.ds(((c % 2) * 2 + po) * TR, TR), :] = value.astype(BF16)

    for d in FAR_X:
        start(early, col_send.at[(x + d) % NX], col_x.at[d - 1], cx_send + d - 1, cx_recv + d - 1, at_x(d))

    for a, cond in enumerate((jnp.logical_not(source), z > r)):
        @pl.when(cond)
        def _():
            arrived(sig_own.at[a], z_recv + a)

        round_x(a, cond)

    tz_send, tz_recv = slots("send", 7), slots("recv", 7)
    for d in range(1, NX):
        arrived(tot_x.at[0], tx_recv + d - 1)
    tot_z[z] = tot_x[0] + tot_x[1] + tot_x[2] + tot_x[3]
    for d in FAR_Z:
        start(None, tot_z.at[z], tot_z.at[z], tz_send + d - 1, tz_recv + d - 1, at_z(d))

    cz_send, cz_recv = slots("send", 7), slots("recv", 7)

    @pl.when(early)
    def _():
        for d in range(1, NX):
            arrived(col_x.at[d - 1], cx_recv + d - 1)
        total = col_send[x].astype(F32)
        for d in range(1, NX):
            total = total + col_x[d - 1].astype(F32)
        for j in range(OWNERS):
            colz_send[j] = total[j * 32 : j * 32 + 32]

    for d in FAR_Z:
        to = (z + d) % NZ
        start(
            early & (to < OWNERS), colz_send.at[lax.rem(to, OWNERS)], col_z.at[d - 1], cz_send + d - 1, cz_recv + d - 1, at_z(d)
        )

    one_load.wait()
    two_load.wait()

    def left_matrix(a):
        blocks = [
            jnp.dot(sig_all[a, j], onev[...], preferred_element_type=F32).astype(BF16) for j in range(NX)
        ]
        parts = []
        for p in range(2):
            gathered = jnp.concatenate(
                [
                    jnp.concatenate([b[p * 32 : p * 32 + 32, q * 128 : q * 128 + 128] for b in blocks], axis=1)
                    for q in range(4)
                ],
                axis=0,
            )
            parts.append(jnp.dot(gathered, twov[...], preferred_element_type=F32))
        lmat[pl.ds(0, 128), pl.ds(0, 384)] = parts[0].astype(BF16)
        lmat[pl.ds(0, 128), pl.ds(384, 384)] = (-parts[1]).astype(BF16)
        lmat[pl.ds(128, 128), pl.ds(0, 384)] = parts[1].astype(BF16)
        lmat[pl.ds(128, 128), pl.ds(384, 384)] = parts[0].astype(BF16)

    s_row = lax.broadcasted_iota(jnp.int32, (TR, 128), 0)

    def contract(ref, masked, half):
        def step(index, carry):
            pair = half * 3 + index
            cols = []
            for j in range(2):
                t = pair * 2 + j
                blocks = [ref[p, t, :, pl.ds(c * 128, 128)] for p in range(2) for c in range(8)]
                if masked:
                    keep = s_row <= h * TP + t - r * TR
                    blocks = [jnp.where(keep, b, jnp.zeros((), BF16)) for b in blocks]
                cols.append(jnp.concatenate(blocks, axis=0))
            out = jnp.dot(lmat[...], jnp.concatenate(cols, axis=1), preferred_element_type=F32) * weight
            for j in range(2):
                for po in range(2):
                    def block(q, b):
                        first = po * 128 + q * 32 + b * 8
                        return out[first : first + 8, j * 128 : j * 128 + 128]

                    total = by_group([block(q, q) for q in range(4)])
                    for d in range(1, 4):
                        moved = by_group([block(q, (q + d) % 4) for q in range(4)])
                        total = total + pltpu.roll(moved, 32 * d, 1)
                    at = (pair * 2 + j) * 2 + po
                    if masked:
                        fpart[at] += total
                    else:
                        fpart[at] = total
            return carry

        lax.fori_loop(0, TP // 4, step, 0, unroll=True)

    les_load.wait()
    for d in range(1, NX):
        arrived(sig_own.at[0], sx_recv + d - 1)
    left_matrix(0)
    contract(lesv, False, 1 - core)
    contract(lesv, False, core)
    cg_send, cg_recv = slots("send", 7), slots("recv", 7)
    owner = z < OWNERS

    @pl.when(owner)
    def _():
        @pl.when(early)
        def _():
            col_own[...] = colz_send[lax.rem(z, OWNERS)]

        @pl.when(jnp.logical_not(early))
        def _():
            col_own[...] = jnp.zeros_like(col_own)

        for d in range(1, NZ):
            @pl.when((z - d + NZ) % NZ <= r)
            def _():
                arrived(col_z.at[d - 1], cz_recv + d - 1)
                col_own[...] += col_z[d - 1]

        col_all[x, lax.rem(z, OWNERS)] = col_own[...].astype(BF16)

    piece = col_all.at[x, lax.rem(z, OWNERS)]
    for d in FAR_Z:
        start(owner, piece, piece, cg_send + d - 1, cg_recv + d - 1, at_z(d))

    adv_load.wait()

    @pl.when(late)
    def _():
        for d in range(1, NX):
            arrived(sig_own.at[1], sx_recv + 3 + d - 1)
        left_matrix(1)
        contract(advv, True, 1 - core)

    rc_send, rc_recv = slots("send", 1), slots("recv", 1)
    start(None, fpart.at[pl.ds(TP * (1 - core), TP)], rs_buf, rc_send, rc_recv, at_core())

    @pl.when(late)
    def _():
        contract(advv, True, core)

    arrived(rs_buf, rc_recv)
    ry_send, ry_recv = slots("send", 7), slots("recv", 7)
    half = fpart[pl.ds(TP * core, TP)] + rs_buf[...]
    y_buf[r] = half.reshape(TP * 8, 128).astype(BF16)
    for d in FAR_R:
        start(None, y_buf.at[r], y_buf.at[r], ry_send + d - 1, ry_recv + d - 1, at_r(d))

    for d in range(1, NZ):
        arrived(tot_z.at[0], tz_recv + d - 1)
    above = jnp.zeros((8, 128), F32)
    for j in range(NZ):
        above = above + jnp.where(j > z, tot_z[j], 0.0)
    for j in range(NX):
        above = above + jnp.where(j > x, tot_x[j], 0.0)
    row_i = lax.broadcasted_iota(jnp.int32, (TP, TP), 0)
    later = jnp.where(lax.broadcasted_iota(jnp.int32, (TP, TP), 1) >= row_i, 1.0, 0.0)
    summed = jnp.dot(later, logs, precision=HIGHEST, preferred_element_type=F32) + above[0:1, 0:64]
    magnitude = jnp.exp(summed[:, 0:32])
    angle = summed[:, 32:64]
    factor = jnp.concatenate([magnitude * jnp.cos(angle), -magnitude * jnp.sin(angle)], axis=0)
    spread = jnp.where(
        lax.broadcasted_iota(jnp.int32, (32, 1024), 1) // 32 == lax.broadcasted_iota(jnp.int32, (32, 1024), 0), 1.0, 0.0
    )
    spread = jnp.dot(factor, spread, precision=HIGHEST, preferred_element_type=F32)
    for c in range(8):
        facv[pl.ds(c, 2 * TP, stride=8), :] = spread[:, c * 128 : c * 128 + 128]

    ca_send, ca_recv = slots("send", 3), slots("recv", 3)
    for d in range(1, NZ):
        @pl.when((z - d + NZ) % NZ < OWNERS)
        def _():
            arrived(col_all.at[0, 0], cg_recv + d - 1)
    for d in FAR_X:
        start(None, col_all.at[x], col_all.at[x], ca_send + d - 1, ca_recv + d - 1, at_x(d))

    for d in range(1, NR):
        arrived(y_buf.at[0], ry_recv + d - 1)
    halves = []
    for k in range(2):
        half = y_buf[k].astype(F32)
        for j in range(k + 2, NR, 2):
            half = half + y_buf[j].astype(F32)
        halves.append(half)

    squares = jnp.zeros((8, 128), F32)
    for t in range(TP):
        fr, fi = facv[pl.ds(t * 8, 8), :], facv[pl.ds((TP + t) * 8, 8), :]
        ar = xv[pl.ds(t * 16, 8, stride=2), :] + halves[t // 6][t % 6 * 16 : t % 6 * 16 + 8]
        ai = xv[pl.ds(t * 16 + 1, 8, stride=2), :] + halves[t // 6][t % 6 * 16 + 8 : t % 6 * 16 + 16]
        step_r, step_i = fr * ar - fi * ai, fr * ai + fi * ar
        stepv[2 * t] = step_r
        stepv[2 * t + 1] = step_i
        squares = squares + (step_r * step_r + step_i * step_i)
    norms[h] = jnp.sum(squares, axis=0, keepdims=True)
    n_send, n_recv = slots("send", NH - 1), slots("recv", NH - 1)
    for k, d in enumerate(FAR_H):
        start(None, norms.at[h], norms.at[h], n_send + k, n_recv + k, at_h(d))

    for k in range(NH - 1):
        arrived(norms.at[0], n_recv + k)
    total = jnp.sum(norms[...], axis=0)
    total = jnp.sum(total, axis=1, keepdims=True)
    scale = 1.0 / jnp.sqrt(total / float(2 * NX * NZ * TP * 1024) + 1e-6)
    for t in range(TP):
        out_ref[pl.ds(t * 16, 8, stride=2), :] = stepv[2 * t] * scale
        out_ref[pl.ds(t * 16 + 1, 8, stride=2), :] = stepv[2 * t + 1] * scale

    for d in range(1, NX):
        arrived(col_all.at[0], ca_recv + d - 1)
    for j in range(NX):
        rows = col_all[j].reshape(4 * TR, 128)
        for c in range(2):
            for po in range(2):
                first = (2 * c + po) * TR
                col_ref[po, :, pl.ds((2 * j + c) * 128, 128)] = rows[first : first + TR]

    for cond, args in pending:
        if cond is None:
            copy(*args).wait_send()
        else:
            @pl.when(cond)
            def _():
                copy(*args).wait_send()
    assert counts["send"] <= SENDS and counts["recv"] <= RECVS, counts


def finish(step_ref, col_ref, step_out, col_out, wide, sems):
    step = pltpu.make_async_copy(step_ref, step_out, sems.at[0])
    step.start()
    copies = []
    for p in range(2):
        wide[p] = col_ref[p].astype(F32)
        copies.append(pltpu.make_async_copy(wide.at[p], col_out.at[p], sems.at[1 + p]))
        copies[p].start()
    for copy in copies:
        copy.wait()
    step.wait()


SENDS = 112
RECVS = 96


def shards(row_less, row_great, coupling, damping, phases, lesser_hist, advanced_hist, retarded_hist):
    def rows(a):
        a = a.transpose(1, 0, 2).reshape(TP, 2, 8, 128)
        return a.transpose(0, 2, 1, 3).reshape(TP * 16, 128)

    one, two, three = (jnp.asarray(m, BF16) for m in lane_order())
    anywhere = pl.BlockSpec(memory_space=pltpu.HBM)
    vmem = pl.BlockSpec(memory_space=pltpu.VMEM)
    scratch = [
        pltpu.VMEM((TP * 16, 128), F32),
        pltpu.VMEM((TP * 16, 128), F32),
        pltpu.VMEM((32, 32), F32),
        pltpu.VMEM((TP, 32), F32),
        pltpu.VMEM((TP, 32), F32),
        pltpu.VMEM((2, TP, TR, 1024), BF16),
        pltpu.VMEM((2, TP, TR, 1024), BF16),
        pltpu.VMEM((2, TP, TR, 1024), BF16),
        pltpu.VMEM((TP * 32, 512), BF16),
        pltpu.VMEM((NX * 128, 8 * TR), BF16),
        pltpu.VMEM((128, 128), BF16),
        pltpu.VMEM((2, 64, TP * 32), BF16),
        pltpu.VMEM((2, NX, 64, TP * 32), BF16),
        pltpu.VMEM((TP // 4, 256, 1024), BF16),
        pltpu.VMEM((8 * TR, 256), F32),
        pltpu.VMEM((NX, 4 * TR, 128), BF16),
        pltpu.VMEM((NX - 1, 4 * TR, 128), BF16),
        pltpu.VMEM((OWNERS, 32, 128), F32),
        pltpu.VMEM((NZ - 1, 32, 128), F32),
        pltpu.VMEM((32, 128), F32),
        pltpu.VMEM((NX, OWNERS, 32, 128), BF16),
        pltpu.VMEM((256, 768), BF16),
        pltpu.VMEM((2 * TP, 8, 128), F32),
        pltpu.VMEM((TP, 8, 128), F32),
        pltpu.VMEM((NR, TP * 8, 128), BF16),
        pltpu.VMEM((NX, 8, 128), F32),
        pltpu.VMEM((NZ, 8, 128), F32),
        pltpu.VMEM((NH, 1, 128), F32),
        pltpu.VMEM((2 * TP * 8, 128), F32),
        pltpu.VMEM((2 * TP, 8, 128), F32),
        pltpu.SemaphoreType.DMA((11,)),
        pltpu.SemaphoreType.DMA((SENDS,)),
        pltpu.SemaphoreType.DMA((RECVS,)),
    ]
    operands = (
        rows(row_less), rows(row_great), coupling, damping, phases,
        lesser_hist.transpose(0, 2, 1, 3), advanced_hist.transpose(0, 2, 1, 3), retarded_hist.transpose(0, 2, 1, 3),
        one, two, three,
    )
    stepped, column = pl.pallas_call(
        body,
        out_shape=(
            jax.ShapeDtypeStruct((TP * 16, 128), F32),
            jax.ShapeDtypeStruct((2, TR, 1024), BF16),
        ),
        in_specs=[anywhere] * 11,
        out_specs=(vmem, vmem),
        scratch_shapes=scratch,
        compiler_params=pltpu.CompilerParams(
            collective_id=0, has_side_effects=True, vmem_limit_bytes=24 * 1024 * 1024
        ),
        name="kadanoff_baym_step",
    )(
        *(pltpu.with_memory_space_constraint(a, pltpu.HBM) for a in operands)
    )
    stepped, column = pl.pallas_call(
        finish,
        out_shape=(jax.ShapeDtypeStruct((TP * 16, 128), F32), jax.ShapeDtypeStruct((2, TR, 1024), F32)),
        in_specs=[vmem, vmem],
        out_specs=(pl.BlockSpec(memory_space=pltpu.HBM),) * 2,
        scratch_shapes=[pltpu.VMEM((2, TR, 1024), F32), pltpu.SemaphoreType.DMA((3,))],
        compiler_params=pltpu.CompilerParams(vmem_limit_bytes=4 * 1024 * 1024),
        name="finish",
    )(stepped, column)
    return stepped.reshape(TP, 8, 2, 128).transpose(2, 0, 1, 3).reshape(2, TP, 1024), column


def solution(mesh):
    return jax.shard_map(
        shards,
        mesh=mesh,
        in_specs=(
            P(None, "hist", None),
            P(None, "hist", None),
            P(),
            P("hist", None),
            P("hist", None),
            P(None, "row", "hist", None),
            P(None, "row", "hist", None),
            P(None, "row", "hist", None),
        ),
        out_specs=(P(None, "hist", None), P(None, "row", None)),
        check_vma=False,
    )
```

```python
import functools

import jax
import jax.numpy as jnp
import numpy as np
from jax import lax
from jax.experimental import pallas as pl
from jax.experimental.pallas import tpu as pltpu
from jax.sharding import PartitionSpec as P

MESH = pl.DeviceIdType.MESH
F32 = jnp.float32
BF16 = jnp.bfloat16
HIGHEST = lax.Precision.HIGHEST
NX = 4
NZ = 8
NR = 8
NH = NX * NZ


def ring(n, d):
    return min(d, n - d)


SPREAD = {0: 4, 1: 5, 2: 3, 3: 6, 4: 1, 5: 0, 6: 2, 7: 7}
FAR_X = sorted(range(1, NX), key=lambda d: -ring(NX, d))
FAR_Z = sorted(range(1, NZ), key=lambda d: -ring(NZ, d))
FAR_R = sorted(range(1, NR), key=lambda d: -ring(NR, d))
FAR_H = sorted(
    ((dz, dx) for dz in range(NZ) for dx in range(NX) if dz or dx), key=lambda d: -ring(NZ, d[0]) - ring(NX, d[1])
)
TP = 12
TR = 48
OWNERS = 6
LANES_TO_LANES = (((1,), (1,)), ((), ()))


def lane_order():
    one = np.zeros((TP * 32, 4 * 128), np.float32)
    two = np.zeros((NX * 128, 8 * TR), np.float32)
    for s in range(TP):
        for c in range(8):
            for q in range(4):
                one[s * 32 + 4 * c + q, q * 128 + c * TP + s] = 1
            for x in range(NX):
                two[x * 128 + c * TP + s, c * TR + x * TP + s] = 1
    three = np.zeros((128, 128), np.float32)
    for q in range(4):
        for a in range(4):
            for c in range(8):
                three[q * 32 + a * 8 + c, q * 32 + 4 * c + a] = 1
    return one, two, three


def body(
    x_hbm, y_hbm, c_hbm, damp_hbm, phase_hbm, les_hbm, adv_hbm, ret_hbm, one_hbm, two_hbm, three_hbm,
    out_ref, col_ref,
    xv, yv, cv, dampv, phasev, lesv, advv, retv, onev, twov, threev,
    sig_own, sig_all, bmat, col_acc, col_send, col_x, colz_send, col_z, col_own, col_all,
    lmat, fpart, rs_buf, y_buf, tot_x, tot_z, norms, facv, stepv,
    load_sem, send_sem, recv_sem,
):
    h = lax.axis_index("hist")
    r = lax.axis_index("row")
    z, x = h // NX, h % NX
    y, core = r // 2, r % 2
    dz = (z - r + NZ) % NZ
    early = z <= r
    source = z == r
    place = (y - z // 2 + 4) % 4 * 2 + (core + z) % 2
    late = z >= r

    def at_x(d):
        return {"hist": z * NX + (x + d) % NX}

    def at_z(d):
        return {"hist": ((z + d + NZ) % NZ) * NX + x}

    def at_h(d):
        return {"hist": (z + d[0]) % NZ * NX + (x + d[1]) % NX}

    def at_core():
        return {"row": 2 * y + 1 - core}

    def at_r(d):
        return {"row": (r + d) % NR}

    counts = {"send": 0, "recv": 0}
    pending = []

    def slots(kind, n):
        first = counts[kind]
        counts[kind] += n
        return first

    def copy(src, dst, send, recv, device):
        return pltpu.make_async_remote_copy(
            src_ref=src, dst_ref=dst, send_sem=send_sem.at[send], recv_sem=recv_sem.at[recv],
            device_id=device, device_id_type=MESH,
        )

    def start(cond, *args):
        if cond is None:
            copy(*args).start()
        else:
            @pl.when(cond)
            def _():
                copy(*args).start()
        pending.append((cond, args))

    def arrived(ref, recv):
        copy(ref, ref, 0, recv, at_x(1)).wait_recv()

    def drain():
        for cond, args in pending:
            if cond is None:
                copy(*args).wait_send()
            else:
                @pl.when(cond)
                def _():
                    copy(*args).wait_send()
        pending.clear()

    loads = []
    for src, dst in (
        (c_hbm, cv), (x_hbm, xv), (y_hbm, yv), (damp_hbm, dampv), (phase_hbm, phasev),
        (one_hbm, onev), (two_hbm, twov), (three_hbm, threev), (ret_hbm, retv), (les_hbm, lesv), (adv_hbm, advv),
    ):
        loads.append(pltpu.make_async_copy(src, dst, load_sem.at[len(loads)]))
        loads[-1].start()
    (c_load, x_load, y_load, damp_load, phase_load, one_load, two_load, three_load, ret_load, les_load, adv_load) = loads

    barrier = pltpu.get_barrier_semaphore()
    for d in range(1, NX):
        pl.semaphore_signal(barrier, inc=1, device_id=at_x(d), device_id_type=MESH)
    for d in range(1, NZ):
        pl.semaphore_signal(barrier, inc=1, device_id=at_z(d), device_id_type=MESH)
    for device in [at_r(d) for d in range(1, NR)]:
        pl.semaphore_signal(barrier, inc=1, device_id=device, device_id_type=MESH)
    for k, d in SPREAD.items():
        @pl.when((z - r + NZ) % NZ == d)
        def _():
            holder = (r // 2 + k // 2) % 4 * 2 + (r + k) % 2
            pl.semaphore_signal(barrier, inc=1, device_id={"hist": r * NX + x, "row": holder}, device_id_type=MESH)

    lane8 = lax.broadcasted_iota(jnp.int32, (8, 128), 1) // 32

    def by_group(parts):
        mask = lane8.reshape((1,) * (parts[0].ndim - 2) + (8, 128))
        out = parts[0]
        for g in range(1, 4):
            out = jnp.where(mask == g, parts[g], out)
        return out

    def rolled(a):
        flat = a.reshape(-1, 128)
        return [a] + [pltpu.roll(flat, 32 * d, 1).reshape(a.shape) for d in range(1, 4)]

    c_load.wait()
    coup = cv[...]
    wide = jnp.concatenate([coup] * 4, axis=1)
    square = jnp.concatenate([wide] * 4, axis=0)
    same = (
        lax.broadcasted_iota(jnp.int32, (128, 128), 0) // 32
        == lax.broadcasted_iota(jnp.int32, (128, 128), 1) // 32
    )
    right = jnp.where(same, square, 0.0)
    rows4 = [cv[pl.ds(g, 8, stride=4), :] for g in range(4)]
    col_of = [[jnp.broadcast_to(rows4[g][:, k : k + 1], (8, 128)) for k in range(32)] for g in range(4)]

    x_load.wait()
    y_load.wait()

    def part(ref, p):
        return ref[pl.ds(p, TP * 8, stride=2), :]

    xr, xi, yr, yi = part(xv, 0), part(xv, 1), part(yv, 0), part(yv, 1)
    polar = jnp.concatenate([-(xr * yr + xi * yi), -(xi * yr - xr * yi)], axis=0)
    half = lax.dot_general(polar, right, LANES_TO_LANES, precision=HIGHEST, preferred_element_type=F32)
    half = half.reshape(2 * TP, 8, 128)
    half_d = rolled(half)
    screen = jnp.zeros((2 * TP, 8, 128), F32)
    for d in range(4):
        for c in range(8):
            factor = by_group([col_of[g][4 * c + (g - d) % 4] for g in range(4)])
            screen = screen + factor[None] * half_d[d][:, c : c + 1, :]
    sr, si = screen[:TP], screen[TP:]
    xr, xi, yr, yi = (a.reshape(TP, 8, 128) for a in (xr, xi, yr, yi))
    less = (xr * sr - xi * si, xr * si + xi * sr)
    great = (yr * sr + yi * si, yi * sr - yr * si)
    ret = (great[0] - less[0], great[1] - less[1])
    less_d = [rolled(a) for a in less]
    for a, pair in enumerate(([rolled(v) for v in ret], less_d)):
        for p in range(2):
            for m in range(3):
                block = jnp.concatenate(
                    [by_group([pair[p][(g - b) % 4][4 * m + g] for g in range(4)]) for b in range(4)], axis=0
                )
                sig_own[a, pl.ds(p * 32, 32), pl.ds(m * 128, 128)] = block.astype(BF16)

    pl.semaphore_wait(barrier, (NX - 1) + (NZ - 1) + (NR - 1) + 1)

    z_send, z_recv = slots("send", 4), slots("recv", 4)
    for a in range(2):
        for half in range(2):
            rows = pl.ds(32 * half, 32)
            for k, d in SPREAD.items():
                if d == 0:
                    continue
                start(
                    (place == k) if a == 0 else (place == k) & ((z + d) % NZ > z),
                    sig_own.at[a, rows], sig_all.at[a, x, rows], z_send + 2 * a + half, z_recv + 2 * a + half,
                    {"hist": (z + d) % NZ * NX + x, "row": z},
                )

    @pl.when(source)
    def _():
        sig_all[:, x] = sig_own[...]

    sx_send, sx_recv = slots("send", 12), slots("recv", 12)

    def round_x(a, half, cond):
        block = sig_all.at[a, x, pl.ds(32 * half, 32)]
        for d in FAR_X:
            at = 6 * a + 3 * half + d - 1
            start(cond, block, block, sx_send + at, sx_recv + at, at_x(d))

    for a in range(2):
        for half in range(2):
            round_x(a, half, source)

    damp_load.wait()
    phase_load.wait()
    logs = jnp.concatenate([jnp.log(dampv[...]), phasev[...]], axis=1)
    tot = jnp.sum(logs, axis=0, keepdims=True)
    tot = jnp.concatenate([tot, jnp.zeros((1, 64), F32)], axis=1)
    tot_x[x] = jnp.broadcast_to(tot, (8, 128))

    tx_send, tx_recv = slots("send", 3), slots("recv", 3)
    for d in FAR_X:
        start(None, tot_x.at[x], tot_x.at[x], tx_send + d - 1, tx_recv + d - 1, at_x(d))

    @pl.when(early)
    def _():
        def square_of(p, s):
            rows = []
            for g in range(4):
                for b in range(4):
                    rows.append(jnp.where(lane8 == g, less_d[p][(g - b) % 4][s], 0.0))
            return jnp.concatenate(rows, axis=0)

        for s in range(TP):
            b0, b1 = square_of(0, s), square_of(1, s)
            bmat[s // 4, pl.ds(0, 128), pl.ds(s % 4 * 256, 128)] = b0.astype(BF16)
            bmat[s // 4, pl.ds(0, 128), pl.ds(s % 4 * 256 + 128, 128)] = b1.astype(BF16)
            bmat[s // 4, pl.ds(128, 128), pl.ds(s % 4 * 256, 128)] = (-b1).astype(BF16)
            bmat[s // 4, pl.ds(128, 128), pl.ds(s % 4 * 256 + 128, 128)] = b0.astype(BF16)

    weight = float(NX * NZ * TP * 32) ** -0.5
    ret_load.wait()
    three_load.wait()
    cx_send, cx_recv = slots("send", 3), slots("recv", 3)

    @pl.when(early)
    def _():
        t_row = lax.broadcasted_iota(jnp.int32, (TR, 128), 0)
        col_acc[...] = jnp.zeros_like(col_acc)

        def step(group, carry):
            rows = []
            for c in range(8):
                lanes = []
                for k in range(4):
                    at = group * 4 + k
                    keep = t_row >= h * TP + at - r * TR
                    for p in range(2):
                        lanes.append(jnp.where(keep, retv[p, at, :, pl.ds(c * 128, 128)], jnp.zeros((), BF16)))
                rows.append(jnp.concatenate(lanes, axis=1))
            col_acc[...] += lax.dot_general(
                jnp.concatenate(rows, axis=0), bmat[group], LANES_TO_LANES, preferred_element_type=F32
            )
            return carry

        lax.fori_loop(0, TP // 4, step, 0)
        for c in range(8):
            for po in range(2):
                value = (col_acc[pl.ds(c * TR, TR), pl.ds(po * 128, 128)] * -weight).astype(BF16)
                value = jnp.dot(value, threev[...], preferred_element_type=F32)
                col_send[c // 2, pl.ds(((c % 2) * 2 + po) * TR, TR), :] = value.astype(BF16)

    for d in FAR_X:
        start(early, col_send.at[(x + d) % NX], col_x.at[d - 1], cx_send + d - 1, cx_recv + d - 1, at_x(d))

    for a, cond in enumerate((jnp.logical_not(source), z > r)):
        for half in range(2):
            @pl.when(cond)
            def _():
                arrived(sig_own.at[a, pl.ds(0, 32)], z_recv + 2 * a + half)

            round_x(a, half, cond)

    tz_send, tz_recv = slots("send", 7), slots("recv", 7)
    for d in range(1, NX):
        arrived(tot_x.at[0], tx_recv + d - 1)
    tot_z[z] = tot_x[0] + tot_x[1] + tot_x[2] + tot_x[3]
    for d in FAR_Z:
        start(None, tot_z.at[z], tot_z.at[z], tz_send + d - 1, tz_recv + d - 1, at_z(d))

    cz_send, cz_recv = slots("send", 7), slots("recv", 7)

    @pl.when(early)
    def _():
        for d in range(1, NX):
            arrived(col_x.at[d - 1], cx_recv + d - 1)
        total = col_send[x].astype(F32)
        for d in range(1, NX):
            total = total + col_x[d - 1].astype(F32)
        for j in range(OWNERS):
            colz_send[j] = total[j * 32 : j * 32 + 32]

    for d in FAR_Z:
        to = (z + d) % NZ
        start(
            early & (to < OWNERS), colz_send.at[lax.rem(to, OWNERS)], col_z.at[d - 1], cz_send + d - 1, cz_recv + d - 1, at_z(d)
        )

    one_load.wait()
    two_load.wait()

    def left_matrix(a):
        blocks = [
            jnp.dot(sig_all[a, j], onev[...], preferred_element_type=F32).astype(BF16) for j in range(NX)
        ]
        parts = []
        for p in range(2):
            gathered = jnp.concatenate(
                [
                    jnp.concatenate([b[p * 32 : p * 32 + 32, q * 128 : q * 128 + 128] for b in blocks], axis=1)
                    for q in range(4)
                ],
                axis=0,
            )
            parts.append(jnp.dot(gathered, twov[...], preferred_element_type=F32))
        lmat[pl.ds(0, 128), pl.ds(0, 384)] = parts[0].astype(BF16)
        lmat[pl.ds(0, 128), pl.ds(384, 384)] = (-parts[1]).astype(BF16)
        lmat[pl.ds(128, 128), pl.ds(0, 384)] = parts[1].astype(BF16)
        lmat[pl.ds(128, 128), pl.ds(384, 384)] = parts[0].astype(BF16)

    s_row = lax.broadcasted_iota(jnp.int32, (TR, 128), 0)

    def contract(ref, masked, half):
        def step(index, carry):
            pair = half * 3 + index
            cols = []
            for j in range(2):
                t = pair * 2 + j
                blocks = [ref[p, t, :, pl.ds(c * 128, 128)] for p in range(2) for c in range(8)]
                if masked:
                    keep = s_row <= h * TP + t - r * TR
                    blocks = [jnp.where(keep, b, jnp.zeros((), BF16)) for b in blocks]
                cols.append(jnp.concatenate(blocks, axis=0))
            out = jnp.dot(lmat[...], jnp.concatenate(cols, axis=1), preferred_element_type=F32) * weight
            for j in range(2):
                for po in range(2):
                    def block(q, b):
                        first = po * 128 + q * 32 + b * 8
                        return out[first : first + 8, j * 128 : j * 128 + 128]

                    total = by_group([block(q, q) for q in range(4)])
                    for d in range(1, 4):
                        moved = by_group([block(q, (q + d) % 4) for q in range(4)])
                        total = total + pltpu.roll(moved, 32 * d, 1)
                    at = (pair * 2 + j) * 2 + po
                    if masked:
                        fpart[at] += total
                    else:
                        fpart[at] = total
            return carry

        lax.fori_loop(0, TP // 4, step, 0, unroll=True)

    les_load.wait()
    for d in range(1, NX):
        for half in range(2):
            arrived(sig_own.at[0, pl.ds(0, 32)], sx_recv + 3 * half + d - 1)
    left_matrix(0)
    contract(lesv, False, 1 - core)
    contract(lesv, False, core)
    adv_load.wait()

    @pl.when(late)
    def _():
        for d in range(1, NX):
            for half in range(2):
                arrived(sig_own.at[1, pl.ds(0, 32)], sx_recv + 6 + 3 * half + d - 1)
        left_matrix(1)
        contract(advv, True, 1 - core)

    rc_send, rc_recv = slots("send", 1), slots("recv", 1)
    start(None, fpart.at[pl.ds(TP * (1 - core), TP)], rs_buf, rc_send, rc_recv, at_core())

    @pl.when(late)
    def _():
        contract(advv, True, core)

    arrived(rs_buf, rc_recv)
    ry_send, ry_recv = slots("send", 7), slots("recv", 7)
    half = fpart[pl.ds(TP * core, TP)] + rs_buf[...]
    y_buf[r] = half.reshape(TP * 8, 128).astype(BF16)
    for d in FAR_R:
        start(None, y_buf.at[r], y_buf.at[r], ry_send + d - 1, ry_recv + d - 1, at_r(d))

    cg_send, cg_recv = slots("send", 7), slots("recv", 7)
    owner = z < OWNERS

    @pl.when(owner)
    def _():
        @pl.when(early)
        def _():
            col_own[...] = colz_send[lax.rem(z, OWNERS)]

        @pl.when(jnp.logical_not(early))
        def _():
            col_own[...] = jnp.zeros_like(col_own)

        for d in range(1, NZ):
            @pl.when((z - d + NZ) % NZ <= r)
            def _():
                arrived(col_z.at[d - 1], cz_recv + d - 1)
                col_own[...] += col_z[d - 1]

        col_all[x, lax.rem(z, OWNERS)] = col_own[...].astype(BF16)

    piece = col_all.at[x, lax.rem(z, OWNERS)]
    for d in FAR_Z:
        start(owner, piece, piece, cg_send + d - 1, cg_recv + d - 1, at_z(d))

    for d in range(1, NZ):
        arrived(tot_z.at[0], tz_recv + d - 1)
    above = jnp.zeros((8, 128), F32)
    for j in range(NZ):
        above = above + jnp.where(j > z, tot_z[j], 0.0)
    for j in range(NX):
        above = above + jnp.where(j > x, tot_x[j], 0.0)
    row_i = lax.broadcasted_iota(jnp.int32, (TP, TP), 0)
    later = jnp.where(lax.broadcasted_iota(jnp.int32, (TP, TP), 1) >= row_i, 1.0, 0.0)
    summed = jnp.dot(later, logs, precision=HIGHEST, preferred_element_type=F32) + above[0:1, 0:64]
    magnitude = jnp.exp(summed[:, 0:32])
    angle = summed[:, 32:64]
    factor = jnp.concatenate([magnitude * jnp.cos(angle), -magnitude * jnp.sin(angle)], axis=0)
    spread = jnp.where(
        lax.broadcasted_iota(jnp.int32, (32, 1024), 1) // 32 == lax.broadcasted_iota(jnp.int32, (32, 1024), 0), 1.0, 0.0
    )
    spread = jnp.dot(factor, spread, precision=HIGHEST, preferred_element_type=F32)
    for c in range(8):
        facv[pl.ds(c, 2 * TP, stride=8), :] = spread[:, c * 128 : c * 128 + 128]

    for d in range(1, NR):
        arrived(y_buf.at[0], ry_recv + d - 1)
    halves = []
    for k in range(2):
        half = y_buf[k].astype(F32)
        for j in range(k + 2, NR, 2):
            half = half + y_buf[j].astype(F32)
        halves.append(half)

    squares = jnp.zeros((8, 128), F32)
    for t in range(TP):
        fr, fi = facv[pl.ds(t * 8, 8), :], facv[pl.ds((TP + t) * 8, 8), :]
        ar = xv[pl.ds(t * 16, 8, stride=2), :] + halves[t // 6][t % 6 * 16 : t % 6 * 16 + 8]
        ai = xv[pl.ds(t * 16 + 1, 8, stride=2), :] + halves[t // 6][t % 6 * 16 + 8 : t % 6 * 16 + 16]
        step_r, step_i = fr * ar - fi * ai, fr * ai + fi * ar
        stepv[2 * t] = step_r
        stepv[2 * t + 1] = step_i
        squares = squares + (step_r * step_r + step_i * step_i)
    norms[h] = jnp.sum(squares, axis=0, keepdims=True)
    n_send, n_recv = slots("send", 1), slots("recv", 1)
    for d in FAR_H:
        copy(norms.at[h], norms.at[h], n_send, n_recv, at_h(d)).start()

    ca_send, ca_recv = slots("send", 3), slots("recv", 3)
    for d in range(1, NZ):
        @pl.when((z - d + NZ) % NZ < OWNERS)
        def _():
            arrived(col_all.at[0, 0], cg_recv + d - 1)
    for d in FAR_X:
        start(None, col_all.at[x], col_all.at[x], ca_send + d - 1, ca_recv + d - 1, at_x(d))

    for d in range(1, NX):
        arrived(col_all.at[0], ca_recv + d - 1)
    for j in range(NX):
        rows = col_all[j].reshape(4 * TR, 128)
        for c in range(2):
            for po in range(2):
                first = (2 * c + po) * TR
                col_ref[po, :, pl.ds((2 * j + c) * 128, 128)] = rows[first : first + TR]
    drain()

    others = norms.at[pl.ds(0, NH - 1)]
    copy(others, others, n_send, n_recv, at_x(1)).wait()
    total = jnp.sum(norms[...], axis=0)
    total = jnp.sum(total, axis=1, keepdims=True)
    scale = 1.0 / jnp.sqrt(total / float(2 * NX * NZ * TP * 1024) + 1e-6)
    for t in range(TP):
        out_ref[pl.ds(t * 16, 8, stride=2), :] = stepv[2 * t] * scale
        out_ref[pl.ds(t * 16 + 1, 8, stride=2), :] = stepv[2 * t + 1] * scale

    assert counts["send"] <= SENDS and counts["recv"] <= RECVS, counts


def finish(step_ref, col_ref, step_out, col_out, wide, sems):
    step = pltpu.make_async_copy(step_ref, step_out, sems.at[0])
    step.start()
    copies = []
    for p in range(2):
        wide[p] = col_ref[p].astype(F32)
        copies.append(pltpu.make_async_copy(wide.at[p], col_out.at[p], sems.at[1 + p]))
        copies[p].start()
    for copy in copies:
        copy.wait()
    step.wait()


SENDS = 112
RECVS = 96


def shards(row_less, row_great, coupling, damping, phases, lesser_hist, advanced_hist, retarded_hist):
    def rows(a):
        a = a.transpose(1, 0, 2).reshape(TP, 2, 8, 128)
        return a.transpose(0, 2, 1, 3).reshape(TP * 16, 128)

    one, two, three = (jnp.asarray(m, BF16) for m in lane_order())
    anywhere = pl.BlockSpec(memory_space=pltpu.HBM)
    vmem = pl.BlockSpec(memory_space=pltpu.VMEM)
    scratch = [
        pltpu.VMEM((TP * 16, 128), F32),
        pltpu.VMEM((TP * 16, 128), F32),
        pltpu.VMEM((32, 32), F32),
        pltpu.VMEM((TP, 32), F32),
        pltpu.VMEM((TP, 32), F32),
        pltpu.VMEM((2, TP, TR, 1024), BF16),
        pltpu.VMEM((2, TP, TR, 1024), BF16),
        pltpu.VMEM((2, TP, TR, 1024), BF16),
        pltpu.VMEM((TP * 32, 512), BF16),
        pltpu.VMEM((NX * 128, 8 * TR), BF16),
        pltpu.VMEM((128, 128), BF16),
        pltpu.VMEM((2, 64, TP * 32), BF16),
        pltpu.VMEM((2, NX, 64, TP * 32), BF16),
        pltpu.VMEM((TP // 4, 256, 1024), BF16),
        pltpu.VMEM((8 * TR, 256), F32),
        pltpu.VMEM((NX, 4 * TR, 128), BF16),
        pltpu.VMEM((NX - 1, 4 * TR, 128), BF16),
        pltpu.VMEM((OWNERS, 32, 128), F32),
        pltpu.VMEM((NZ - 1, 32, 128), F32),
        pltpu.VMEM((32, 128), F32),
        pltpu.VMEM((NX, OWNERS, 32, 128), BF16),
        pltpu.VMEM((256, 768), BF16),
        pltpu.VMEM((2 * TP, 8, 128), F32),
        pltpu.VMEM((TP, 8, 128), F32),
        pltpu.VMEM((NR, TP * 8, 128), BF16),
        pltpu.VMEM((NX, 8, 128), F32),
        pltpu.VMEM((NZ, 8, 128), F32),
        pltpu.VMEM((NH, 1, 128), F32),
        pltpu.VMEM((2 * TP * 8, 128), F32),
        pltpu.VMEM((2 * TP, 8, 128), F32),
        pltpu.SemaphoreType.DMA((11,)),
        pltpu.SemaphoreType.DMA((SENDS,)),
        pltpu.SemaphoreType.DMA((RECVS,)),
    ]
    operands = (
        rows(row_less), rows(row_great), coupling, damping, phases,
        lesser_hist.transpose(0, 2, 1, 3), advanced_hist.transpose(0, 2, 1, 3), retarded_hist.transpose(0, 2, 1, 3),
        one, two, three,
    )
    stepped, column = pl.pallas_call(
        body,
        out_shape=(
            jax.ShapeDtypeStruct((TP * 16, 128), F32),
            jax.ShapeDtypeStruct((2, TR, 1024), BF16),
        ),
        in_specs=[anywhere] * 11,
        out_specs=(vmem, vmem),
        scratch_shapes=scratch,
        compiler_params=pltpu.CompilerParams(
            collective_id=0, has_side_effects=True, vmem_limit_bytes=24 * 1024 * 1024
        ),
        name="kadanoff_baym_step",
    )(
        *(pltpu.with_memory_space_constraint(a, pltpu.HBM) for a in operands)
    )
    stepped, column = pl.pallas_call(
        finish,
        out_shape=(jax.ShapeDtypeStruct((TP * 16, 128), F32), jax.ShapeDtypeStruct((2, TR, 1024), F32)),
        in_specs=[vmem, vmem],
        out_specs=(pl.BlockSpec(memory_space=pltpu.HBM),) * 2,
        scratch_shapes=[pltpu.VMEM((2, TR, 1024), F32), pltpu.SemaphoreType.DMA((3,))],
        compiler_params=pltpu.CompilerParams(vmem_limit_bytes=4 * 1024 * 1024),
        name="finish",
    )(stepped, column)
    return stepped.reshape(TP, 8, 2, 128).transpose(2, 0, 1, 3).reshape(2, TP, 1024), column


def solution(mesh):
    return jax.shard_map(
        shards,
        mesh=mesh,
        in_specs=(
            P(None, "hist", None),
            P(None, "hist", None),
            P(),
            P("hist", None),
            P("hist", None),
            P(None, "row", "hist", None),
            P(None, "row", "hist", None),
            P(None, "row", "hist", None),
        ),
        out_specs=(P(None, "hist", None), P(None, "row", None)),
        check_vma=False,
    )
```

```python
import functools

import jax
import jax.numpy as jnp
import numpy as np
from jax import lax
from jax.experimental import pallas as pl
from jax.experimental.pallas import tpu as pltpu
from jax.sharding import PartitionSpec as P

MESH = pl.DeviceIdType.MESH
F32 = jnp.float32
BF16 = jnp.bfloat16
HIGHEST = lax.Precision.HIGHEST
NX = 4
NZ = 8
NR = 8
NH = NX * NZ


def ring(n, d):
    return min(d, n - d)


SPREAD = {0: 4, 1: 5, 2: 3, 3: 6, 4: 1, 5: 0, 6: 2, 7: 7}
FAR_X = sorted(range(1, NX), key=lambda d: -ring(NX, d))
FAR_Z = sorted(range(1, NZ), key=lambda d: -ring(NZ, d))
FAR_R = sorted(range(1, NR), key=lambda d: -ring(NR, d))
FAR_H = sorted(
    ((dz, dx) for dz in range(NZ) for dx in range(NX) if dz or dx), key=lambda d: -ring(NZ, d[0]) - ring(NX, d[1])
)
TP = 12
TR = 48
OWNERS = 6
LANES_TO_LANES = (((1,), (1,)), ((), ()))


def lane_order():
    one = np.zeros((TP * 32, 4 * 128), np.float32)
    two = np.zeros((NX * 128, 8 * TR), np.float32)
    for s in range(TP):
        for c in range(8):
            for q in range(4):
                one[s * 32 + 4 * c + q, q * 128 + c * TP + s] = 1
            for x in range(NX):
                two[x * 128 + c * TP + s, c * TR + x * TP + s] = 1
    three = np.zeros((128, 128), np.float32)
    for q in range(4):
        for a in range(4):
            for c in range(8):
                three[q * 32 + a * 8 + c, q * 32 + 4 * c + a] = 1
    return one, two, three


def body(
    x_hbm, y_hbm, c_hbm, damp_hbm, phase_hbm, les_hbm, adv_hbm, ret_hbm, one_hbm, two_hbm, three_hbm,
    out_ref, col_ref,
    xv, yv, cv, dampv, phasev, lesv, advv, retv, onev, twov, threev,
    sig_own, sig_all, bmat, col_acc, col_send, col_x, colz_send, col_z, col_own, col_all,
    lmat, fpart, rs_buf, y_buf, tot_x, tot_z, norms, facv, stepv,
    load_sem, send_sem, recv_sem,
):
    h = lax.axis_index("hist")
    r = lax.axis_index("row")
    z, x = h // NX, h % NX
    y, core = r // 2, r % 2
    dz = (z - r + NZ) % NZ
    early = z <= r
    source = z == r
    place = (y - z // 2 + 4) % 4 * 2 + (core + z) % 2
    late = z >= r

    def at_x(d):
        return {"hist": z * NX + (x + d) % NX}

    def at_z(d):
        return {"hist": ((z + d + NZ) % NZ) * NX + x}

    def at_h(d):
        return {"hist": (z + d[0]) % NZ * NX + (x + d[1]) % NX}

    def at_core():
        return {"row": 2 * y + 1 - core}

    def at_r(d):
        return {"row": (r + d) % NR}

    counts = {"send": 0, "recv": 0}
    pending = []

    def slots(kind, n):
        first = counts[kind]
        counts[kind] += n
        return first

    def copy(src, dst, send, recv, device):
        return pltpu.make_async_remote_copy(
            src_ref=src, dst_ref=dst, send_sem=send_sem.at[send], recv_sem=recv_sem.at[recv],
            device_id=device, device_id_type=MESH,
        )

    def start(cond, *args):
        if cond is None:
            copy(*args).start()
        else:
            @pl.when(cond)
            def _():
                copy(*args).start()
        pending.append((cond, args))

    def arrived(ref, recv):
        copy(ref, ref, 0, recv, at_x(1)).wait_recv()

    def drain():
        for cond, args in pending:
            if cond is None:
                copy(*args).wait_send()
            else:
                @pl.when(cond)
                def _():
                    copy(*args).wait_send()
        pending.clear()

    loads = []
    for src, dst in (
        (c_hbm, cv), (x_hbm, xv), (y_hbm, yv), (damp_hbm, dampv), (phase_hbm, phasev),
        (one_hbm, onev), (two_hbm, twov), (three_hbm, threev), (ret_hbm, retv), (les_hbm, lesv), (adv_hbm, advv),
    ):
        loads.append(pltpu.make_async_copy(src, dst, load_sem.at[len(loads)]))
        loads[-1].start()
    (c_load, x_load, y_load, damp_load, phase_load, one_load, two_load, three_load, ret_load, les_load, adv_load) = loads

    barrier = pltpu.get_barrier_semaphore()
    for d in range(1, NX):
        pl.semaphore_signal(barrier, inc=1, device_id=at_x(d), device_id_type=MESH)
    for d in range(1, NZ):
        pl.semaphore_signal(barrier, inc=1, device_id=at_z(d), device_id_type=MESH)
    for device in [at_r(d) for d in range(1, NR)]:
        pl.semaphore_signal(barrier, inc=1, device_id=device, device_id_type=MESH)
    for k, d in SPREAD.items():
        @pl.when((z - r + NZ) % NZ == d)
        def _():
            holder = (r // 2 + k // 2) % 4 * 2 + (r + k) % 2
            pl.semaphore_signal(barrier, inc=1, device_id={"hist": r * NX + x, "row": holder}, device_id_type=MESH)

    lane8 = lax.broadcasted_iota(jnp.int32, (8, 128), 1) // 32

    def by_group(parts):
        mask = lane8.reshape((1,) * (parts[0].ndim - 2) + (8, 128))
        out = parts[0]
        for g in range(1, 4):
            out = jnp.where(mask == g, parts[g], out)
        return out

    def rolled(a):
        flat = a.reshape(-1, 128)
        return [a] + [pltpu.roll(flat, 32 * d, 1).reshape(a.shape) for d in range(1, 4)]

    c_load.wait()
    coup = cv[...]
    wide = jnp.concatenate([coup] * 4, axis=1)
    square = jnp.concatenate([wide] * 4, axis=0)
    same = (
        lax.broadcasted_iota(jnp.int32, (128, 128), 0) // 32
        == lax.broadcasted_iota(jnp.int32, (128, 128), 1) // 32
    )
    right = jnp.where(same, square, 0.0)
    rows4 = [cv[pl.ds(g, 8, stride=4), :] for g in range(4)]
    col_of = [[jnp.broadcast_to(rows4[g][:, k : k + 1], (8, 128)) for k in range(32)] for g in range(4)]

    x_load.wait()
    y_load.wait()

    def part(ref, p):
        return ref[pl.ds(p, TP * 8, stride=2), :]

    xr, xi, yr, yi = part(xv, 0), part(xv, 1), part(yv, 0), part(yv, 1)
    polar = jnp.concatenate([-(xr * yr + xi * yi), -(xi * yr - xr * yi)], axis=0)
    half = lax.dot_general(polar, right, LANES_TO_LANES, precision=HIGHEST, preferred_element_type=F32)
    half = half.reshape(2 * TP, 8, 128)
    half_d = rolled(half)
    screen = jnp.zeros((2 * TP, 8, 128), F32)
    for d in range(4):
        for c in range(8):
            factor = by_group([col_of[g][4 * c + (g - d) % 4] for g in range(4)])
            screen = screen + factor[None] * half_d[d][:, c : c + 1, :]
    sr, si = screen[:TP], screen[TP:]
    xr, xi, yr, yi = (a.reshape(TP, 8, 128) for a in (xr, xi, yr, yi))
    less = (xr * sr - xi * si, xr * si + xi * sr)
    great = (yr * sr + yi * si, yi * sr - yr * si)
    ret = (great[0] - less[0], great[1] - less[1])
    less_d = [rolled(a) for a in less]
    for a, pair in enumerate(([rolled(v) for v in ret], less_d)):
        for p in range(2):
            for m in range(3):
                block = jnp.concatenate(
                    [by_group([pair[p][(g - b) % 4][4 * m + g] for g in range(4)]) for b in range(4)], axis=0
                )
                sig_own[a, pl.ds(p * 32, 32), pl.ds(m * 128, 128)] = block.astype(BF16)

    pl.semaphore_wait(barrier, (NX - 1) + (NZ - 1) + (NR - 1) + 1)

    z_send, z_recv = slots("send", 4), slots("recv", 4)
    for a in range(2):
        for half in range(2):
            rows = pl.ds(32 * half, 32)
            for k, d in SPREAD.items():
                if d == 0:
                    continue
                start(
                    (place == k) if a == 0 else (place == k) & ((z + d) % NZ > z),
                    sig_own.at[a, rows], sig_all.at[a, x, rows], z_send + 2 * a + half, z_recv + 2 * a + half,
                    {"hist": (z + d) % NZ * NX + x, "row": z},
                )

    @pl.when(source)
    def _():
        sig_all[:, x] = sig_own[...]

    sx_send, sx_recv = slots("send", 12), slots("recv", 12)

    def round_x(a, half, cond):
        block = sig_all.at[a, x, pl.ds(32 * half, 32)]
        for d in FAR_X:
            at = 6 * a + 3 * half + d - 1
            start(cond, block, block, sx_send + at, sx_recv + at, at_x(d))

    for a in range(2):
        for half in range(2):
            round_x(a, half, source)

    damp_load.wait()
    phase_load.wait()
    logs = jnp.concatenate([jnp.log(dampv[...]), phasev[...]], axis=1)
    tot = jnp.sum(logs, axis=0, keepdims=True)
    tot = jnp.concatenate([tot, jnp.zeros((1, 64), F32)], axis=1)
    tot_x[x] = jnp.broadcast_to(tot, (8, 128))

    tx_send, tx_recv = slots("send", 3), slots("recv", 3)
    for d in FAR_X:
        start(None, tot_x.at[x], tot_x.at[x], tx_send + d - 1, tx_recv + d - 1, at_x(d))

    @pl.when(early)
    def _():
        def square_of(p, s):
            rows = []
            for g in range(4):
                for b in range(4):
                    rows.append(jnp.where(lane8 == g, less_d[p][(g - b) % 4][s], 0.0))
            return jnp.concatenate(rows, axis=0)

        for s in range(TP):
            b0, b1 = square_of(0, s), square_of(1, s)
            bmat[s // 4, pl.ds(0, 128), pl.ds(s % 4 * 256, 128)] = b0.astype(BF16)
            bmat[s // 4, pl.ds(0, 128), pl.ds(s % 4 * 256 + 128, 128)] = b1.astype(BF16)
            bmat[s // 4, pl.ds(128, 128), pl.ds(s % 4 * 256, 128)] = (-b1).astype(BF16)
            bmat[s // 4, pl.ds(128, 128), pl.ds(s % 4 * 256 + 128, 128)] = b0.astype(BF16)

    weight = float(NX * NZ * TP * 32) ** -0.5
    ret_load.wait()
    three_load.wait()
    cx_send, cx_recv = slots("send", 3), slots("recv", 3)

    @pl.when(early)
    def _():
        t_row = lax.broadcasted_iota(jnp.int32, (TR, 128), 0)
        col_acc[...] = jnp.zeros_like(col_acc)

        def step(group, carry):
            rows = []
            for c in range(8):
                lanes = []
                for k in range(4):
                    at = group * 4 + k
                    keep = t_row >= h * TP + at - r * TR
                    for p in range(2):
                        lanes.append(jnp.where(keep, retv[p, at, :, pl.ds(c * 128, 128)], jnp.zeros((), BF16)))
                rows.append(jnp.concatenate(lanes, axis=1))
            col_acc[...] += lax.dot_general(
                jnp.concatenate(rows, axis=0), bmat[group], LANES_TO_LANES, preferred_element_type=F32
            )
            return carry

        lax.fori_loop(0, TP // 4, step, 0)
        for c in range(8):
            for po in range(2):
                value = (col_acc[pl.ds(c * TR, TR), pl.ds(po * 128, 128)] * -weight).astype(BF16)
                value = jnp.dot(value, threev[...], preferred_element_type=F32)
                col_send[c // 2, pl.ds(((c % 2) * 2 + po) * TR, TR), :] = value.astype(BF16)


    for a, cond in enumerate((jnp.logical_not(source), z > r)):
        for half in range(2):
            @pl.when(cond)
            def _():
                arrived(sig_own.at[a, pl.ds(0, 32)], z_recv + 2 * a + half)

            round_x(a, half, cond)

    for d in FAR_X:
        start(early, col_send.at[(x + d) % NX], col_x.at[d - 1], cx_send + d - 1, cx_recv + d - 1, at_x(d))

    tz_send, tz_recv = slots("send", 7), slots("recv", 7)
    for d in range(1, NX):
        arrived(tot_x.at[0], tx_recv + d - 1)
    tot_z[z] = tot_x[0] + tot_x[1] + tot_x[2] + tot_x[3]
    for d in FAR_Z:
        start(None, tot_z.at[z], tot_z.at[z], tz_send + d - 1, tz_recv + d - 1, at_z(d))

    cz_send, cz_recv = slots("send", 7), slots("recv", 7)

    @pl.when(early)
    def _():
        for d in range(1, NX):
            arrived(col_x.at[d - 1], cx_recv + d - 1)
        total = col_send[x].astype(F32)
        for d in range(1, NX):
            total = total + col_x[d - 1].astype(F32)
        for j in range(OWNERS):
            colz_send[j] = total[j * 32 : j * 32 + 32]

    for d in FAR_Z:
        to = (z + d) % NZ
        start(
            early & (to < OWNERS), colz_send.at[lax.rem(to, OWNERS)], col_z.at[d - 1], cz_send + d - 1, cz_recv + d - 1, at_z(d)
        )

    one_load.wait()
    two_load.wait()

    def left_matrix(a):
        blocks = [
            jnp.dot(sig_all[a, j], onev[...], preferred_element_type=F32).astype(BF16) for j in range(NX)
        ]
        parts = []
        for p in range(2):
            gathered = jnp.concatenate(
                [
                    jnp.concatenate([b[p * 32 : p * 32 + 32, q * 128 : q * 128 + 128] for b in blocks], axis=1)
                    for q in range(4)
                ],
                axis=0,
            )
            parts.append(jnp.dot(gathered, twov[...], preferred_element_type=F32))
        lmat[pl.ds(0, 128), pl.ds(0, 384)] = parts[0].astype(BF16)
        lmat[pl.ds(0, 128), pl.ds(384, 384)] = (-parts[1]).astype(BF16)
        lmat[pl.ds(128, 128), pl.ds(0, 384)] = parts[1].astype(BF16)
        lmat[pl.ds(128, 128), pl.ds(384, 384)] = parts[0].astype(BF16)

    s_row = lax.broadcasted_iota(jnp.int32, (TR, 128), 0)

    def contract(ref, masked, half):
        def step(index, carry):
            pair = half * 3 + index
            cols = []
            for j in range(2):
                t = pair * 2 + j
                blocks = [ref[p, t, :, pl.ds(c * 128, 128)] for p in range(2) for c in range(8)]
                if masked:
                    keep = s_row <= h * TP + t - r * TR
                    blocks = [jnp.where(keep, b, jnp.zeros((), BF16)) for b in blocks]
                cols.append(jnp.concatenate(blocks, axis=0))
            out = jnp.dot(lmat[...], jnp.concatenate(cols, axis=1), preferred_element_type=F32) * weight
            for j in range(2):
                for po in range(2):
                    def block(q, b):
                        first = po * 128 + q * 32 + b * 8
                        return out[first : first + 8, j * 128 : j * 128 + 128]

                    total = by_group([block(q, q) for q in range(4)])
                    for d in range(1, 4):
                        moved = by_group([block(q, (q + d) % 4) for q in range(4)])
                        total = total + pltpu.roll(moved, 32 * d, 1)
                    at = (pair * 2 + j) * 2 + po
                    if masked:
                        fpart[at] += total
                    else:
                        fpart[at] = total
            return carry

        lax.fori_loop(0, TP // 4, step, 0, unroll=True)

    les_load.wait()
    for d in range(1, NX):
        for half in range(2):
            arrived(sig_own.at[0, pl.ds(0, 32)], sx_recv + 3 * half + d - 1)
    left_matrix(0)
    contract(lesv, False, 1 - core)
    contract(lesv, False, core)
    adv_load.wait()

    @pl.when(late)
    def _():
        for d in range(1, NX):
            for half in range(2):
                arrived(sig_own.at[1, pl.ds(0, 32)], sx_recv + 6 + 3 * half + d - 1)
        left_matrix(1)
        contract(advv, True, 1 - core)

    rc_send, rc_recv = slots("send", 1), slots("recv", 1)
    start(None, fpart.at[pl.ds(TP * (1 - core), TP)], rs_buf, rc_send, rc_recv, at_core())

    @pl.when(late)
    def _():
        contract(advv, True, core)

    arrived(rs_buf, rc_recv)
    ry_send, ry_recv = slots("send", 7), slots("recv", 7)
    half = fpart[pl.ds(TP * core, TP)] + rs_buf[...]
    y_buf[r] = half.reshape(TP * 8, 128).astype(BF16)
    for d in FAR_R:
        start(None, y_buf.at[r], y_buf.at[r], ry_send + d - 1, ry_recv + d - 1, at_r(d))

    cg_send, cg_recv = slots("send", 7), slots("recv", 7)
    owner = z < OWNERS

    @pl.when(owner)
    def _():
        @pl.when(early)
        def _():
            col_own[...] = colz_send[lax.rem(z, OWNERS)]

        @pl.when(jnp.logical_not(early))
        def _():
            col_own[...] = jnp.zeros_like(col_own)

        for d in range(1, NZ):
            @pl.when((z - d + NZ) % NZ <= r)
            def _():
                arrived(col_z.at[d - 1], cz_recv + d - 1)
                col_own[...] += col_z[d - 1]

        col_all[x, lax.rem(z, OWNERS)] = col_own[...].astype(BF16)

    piece = col_all.at[x, lax.rem(z, OWNERS)]
    for d in FAR_Z:
        start(owner, piece, piece, cg_send + d - 1, cg_recv + d - 1, at_z(d))

    for d in range(1, NZ):
        arrived(tot_z.at[0], tz_recv + d - 1)
    above = jnp.zeros((8, 128), F32)
    for j in range(NZ):
        above = above + jnp.where(j > z, tot_z[j], 0.0)
    for j in range(NX):
        above = above + jnp.where(j > x, tot_x[j], 0.0)
    row_i = lax.broadcasted_iota(jnp.int32, (TP, TP), 0)
    later = jnp.where(lax.broadcasted_iota(jnp.int32, (TP, TP), 1) >= row_i, 1.0, 0.0)
    summed = jnp.dot(later, logs, precision=HIGHEST, preferred_element_type=F32) + above[0:1, 0:64]
    magnitude = jnp.exp(summed[:, 0:32])
    angle = summed[:, 32:64]
    factor = jnp.concatenate([magnitude * jnp.cos(angle), -magnitude * jnp.sin(angle)], axis=0)
    spread = jnp.where(
        lax.broadcasted_iota(jnp.int32, (32, 1024), 1) // 32 == lax.broadcasted_iota(jnp.int32, (32, 1024), 0), 1.0, 0.0
    )
    spread = jnp.dot(factor, spread, precision=HIGHEST, preferred_element_type=F32)
    for c in range(8):
        facv[pl.ds(c, 2 * TP, stride=8), :] = spread[:, c * 128 : c * 128 + 128]

    for d in range(1, NR):
        arrived(y_buf.at[0], ry_recv + d - 1)
    halves = []
    for k in range(2):
        half = y_buf[k].astype(F32)
        for j in range(k + 2, NR, 2):
            half = half + y_buf[j].astype(F32)
        halves.append(half)

    squares = jnp.zeros((8, 128), F32)
    for t in range(TP):
        fr, fi = facv[pl.ds(t * 8, 8), :], facv[pl.ds((TP + t) * 8, 8), :]
        ar = xv[pl.ds(t * 16, 8, stride=2), :] + halves[t // 6][t % 6 * 16 : t % 6 * 16 + 8]
        ai = xv[pl.ds(t * 16 + 1, 8, stride=2), :] + halves[t // 6][t % 6 * 16 + 8 : t % 6 * 16 + 16]
        step_r, step_i = fr * ar - fi * ai, fr * ai + fi * ar
        stepv[2 * t] = step_r
        stepv[2 * t + 1] = step_i
        squares = squares + (step_r * step_r + step_i * step_i)
    norms[h] = jnp.sum(squares, axis=0, keepdims=True)
    n_send, n_recv = slots("send", 1), slots("recv", 1)
    for d in FAR_H:
        copy(norms.at[h], norms.at[h], n_send, n_recv, at_h(d)).start()

    ca_send, ca_recv = slots("send", 3), slots("recv", 3)
    for d in range(1, NZ):
        @pl.when((z - d + NZ) % NZ < OWNERS)
        def _():
            arrived(col_all.at[0, 0], cg_recv + d - 1)
    for d in FAR_X:
        start(None, col_all.at[x], col_all.at[x], ca_send + d - 1, ca_recv + d - 1, at_x(d))

    for d in range(1, NX):
        arrived(col_all.at[0], ca_recv + d - 1)
    for j in range(NX):
        rows = col_all[j].reshape(4 * TR, 128)
        for c in range(2):
            for po in range(2):
                first = (2 * c + po) * TR
                col_ref[po, :, pl.ds((2 * j + c) * 128, 128)] = rows[first : first + TR]
    drain()

    others = norms.at[pl.ds(0, NH - 1)]
    copy(others, others, n_send, n_recv, at_x(1)).wait()
    total = jnp.sum(norms[...], axis=0)
    total = jnp.sum(total, axis=1, keepdims=True)
    scale = 1.0 / jnp.sqrt(total / float(2 * NX * NZ * TP * 1024) + 1e-6)
    for t in range(TP):
        out_ref[pl.ds(t * 16, 8, stride=2), :] = stepv[2 * t] * scale
        out_ref[pl.ds(t * 16 + 1, 8, stride=2), :] = stepv[2 * t + 1] * scale

    assert counts["send"] <= SENDS and counts["recv"] <= RECVS, counts


def finish(step_ref, col_ref, step_out, col_out, wide, sems):
    step = pltpu.make_async_copy(step_ref, step_out, sems.at[0])
    step.start()
    copies = []
    for p in range(2):
        wide[p] = col_ref[p].astype(F32)
        copies.append(pltpu.make_async_copy(wide.at[p], col_out.at[p], sems.at[1 + p]))
        copies[p].start()
    for copy in copies:
        copy.wait()
    step.wait()


SENDS = 55
RECVS = 55


def shards(row_less, row_great, coupling, damping, phases, lesser_hist, advanced_hist, retarded_hist):
    def rows(a):
        a = a.transpose(1, 0, 2).reshape(TP, 2, 8, 128)
        return a.transpose(0, 2, 1, 3).reshape(TP * 16, 128)

    one, two, three = (jnp.asarray(m, BF16) for m in lane_order())
    anywhere = pl.BlockSpec(memory_space=pltpu.HBM)
    vmem = pl.BlockSpec(memory_space=pltpu.VMEM)
    scratch = [
        pltpu.VMEM((TP * 16, 128), F32),
        pltpu.VMEM((TP * 16, 128), F32),
        pltpu.VMEM((32, 32), F32),
        pltpu.VMEM((TP, 32), F32),
        pltpu.VMEM((TP, 32), F32),
        pltpu.VMEM((2, TP, TR, 1024), BF16),
        pltpu.VMEM((2, TP, TR, 1024), BF16),
        pltpu.VMEM((2, TP, TR, 1024), BF16),
        pltpu.VMEM((TP * 32, 512), BF16),
        pltpu.VMEM((NX * 128, 8 * TR), BF16),
        pltpu.VMEM((128, 128), BF16),
        pltpu.VMEM((2, 64, TP * 32), BF16),
        pltpu.VMEM((2, NX, 64, TP * 32), BF16),
        pltpu.VMEM((TP // 4, 256, 1024), BF16),
        pltpu.VMEM((8 * TR, 256), F32),
        pltpu.VMEM((NX, 4 * TR, 128), BF16),
        pltpu.VMEM((NX - 1, 4 * TR, 128), BF16),
        pltpu.VMEM((OWNERS, 32, 128), F32),
        pltpu.VMEM((NZ - 1, 32, 128), F32),
        pltpu.VMEM((32, 128), F32),
        pltpu.VMEM((NX, OWNERS, 32, 128), BF16),
        pltpu.VMEM((256, 768), BF16),
        pltpu.VMEM((2 * TP, 8, 128), F32),
        pltpu.VMEM((TP, 8, 128), F32),
        pltpu.VMEM((NR, TP * 8, 128), BF16),
        pltpu.VMEM((NX, 8, 128), F32),
        pltpu.VMEM((NZ, 8, 128), F32),
        pltpu.VMEM((NH, 1, 128), F32),
        pltpu.VMEM((2 * TP * 8, 128), F32),
        pltpu.VMEM((2 * TP, 8, 128), F32),
        pltpu.SemaphoreType.DMA((11,)),
        pltpu.SemaphoreType.DMA((SENDS,)),
        pltpu.SemaphoreType.DMA((RECVS,)),
    ]
    operands = (
        rows(row_less), rows(row_great), coupling, damping, phases,
        lesser_hist.transpose(0, 2, 1, 3), advanced_hist.transpose(0, 2, 1, 3), retarded_hist.transpose(0, 2, 1, 3),
        one, two, three,
    )
    stepped, column = pl.pallas_call(
        body,
        out_shape=(
            jax.ShapeDtypeStruct((TP * 16, 128), F32),
            jax.ShapeDtypeStruct((2, TR, 1024), BF16),
        ),
        in_specs=[anywhere] * 11,
        out_specs=(vmem, vmem),
        scratch_shapes=scratch,
        compiler_params=pltpu.CompilerParams(
            collective_id=0, has_side_effects=True, vmem_limit_bytes=24 * 1024 * 1024
        ),
        name="kadanoff_baym_step",
    )(
        *(pltpu.with_memory_space_constraint(a, pltpu.HBM) for a in operands)
    )
    stepped, column = pl.pallas_call(
        finish,
        out_shape=(jax.ShapeDtypeStruct((TP * 16, 128), F32), jax.ShapeDtypeStruct((2, TR, 1024), F32)),
        in_specs=[vmem, vmem],
        out_specs=(pl.BlockSpec(memory_space=pltpu.HBM),) * 2,
        scratch_shapes=[pltpu.VMEM((2, TR, 1024), F32), pltpu.SemaphoreType.DMA((3,))],
        compiler_params=pltpu.CompilerParams(vmem_limit_bytes=4 * 1024 * 1024),
        name="finish",
    )(stepped, column)
    return stepped.reshape(TP, 8, 2, 128).transpose(2, 0, 1, 3).reshape(2, TP, 1024), column


def solution(mesh):
    return jax.shard_map(
        shards,
        mesh=mesh,
        in_specs=(
            P(None, "hist", None),
            P(None, "hist", None),
            P(),
            P("hist", None),
            P("hist", None),
            P(None, "row", "hist", None),
            P(None, "row", "hist", None),
            P(None, "row", "hist", None),
        ),
        out_specs=(P(None, "hist", None), P(None, "row", None)),
        check_vma=False,
    )
```

```python
import functools

import jax
import jax.numpy as jnp
import numpy as np
from jax import lax
from jax.experimental import pallas as pl
from jax.experimental.pallas import tpu as pltpu
from jax.sharding import PartitionSpec as P

MESH = pl.DeviceIdType.MESH
F32 = jnp.float32
BF16 = jnp.bfloat16
HIGHEST = lax.Precision.HIGHEST
NX = 4
NZ = 8
NR = 8
NH = NX * NZ


def ring(n, d):
    return min(d, n - d)


SPREAD = {0: 4, 1: 5, 2: 3, 3: 6, 4: 1, 5: 0, 6: 2, 7: 7}
FAR_X = sorted(range(1, NX), key=lambda d: -ring(NX, d))
FAR_Z = sorted(range(1, NZ), key=lambda d: -ring(NZ, d))
FAR_R = sorted(range(1, NR), key=lambda d: -ring(NR, d))
FAR_H = sorted(
    ((dz, dx) for dz in range(NZ) for dx in range(NX) if dz or dx), key=lambda d: -ring(NZ, d[0]) - ring(NX, d[1])
)
TP = 12
TR = 48
OWNERS = 6
LANES_TO_LANES = (((1,), (1,)), ((), ()))


def lane_order():
    one = np.zeros((TP * 32, 4 * 128), np.float32)
    two = np.zeros((NX * 128, 8 * TR), np.float32)
    for s in range(TP):
        for c in range(8):
            for q in range(4):
                one[s * 32 + 4 * c + q, q * 128 + c * TP + s] = 1
            for x in range(NX):
                two[x * 128 + c * TP + s, c * TR + x * TP + s] = 1
    three = np.zeros((128, 128), np.float32)
    for q in range(4):
        for a in range(4):
            for c in range(8):
                three[q * 32 + a * 8 + c, q * 32 + 4 * c + a] = 1
    return one, two, three


def body(
    x_hbm, y_hbm, c_hbm, damp_hbm, phase_hbm, les_hbm, adv_hbm, ret_hbm, one_hbm, two_hbm, three_hbm,
    out_ref, col_ref,
    xv, yv, cv, dampv, phasev, lesv, advv, retv, onev, twov, threev,
    sig_own, sig_all, bmat, col_acc, col_send, col_x, colz_send, col_z, col_own, col_all,
    lmat, fpart, rs_buf, y_buf, tot_x, tot_z, norms, facv, stepv,
    load_sem, send_sem, recv_sem,
):
    h = lax.axis_index("hist")
    r = lax.axis_index("row")
    z, x = h // NX, h % NX
    y, core = r // 2, r % 2
    dz = (z - r + NZ) % NZ
    early = z <= r
    source = z == r
    place = (y - z // 2 + 4) % 4 * 2 + (core + z) % 2
    goes_up = False
    for k, d in SPREAD.items():
        goes_up = goes_up | ((place == k) & ((z + d) % NZ > z))
    late = z >= r

    def at_x(d):
        return {"hist": z * NX + (x + d) % NX}

    def at_z(d):
        return {"hist": ((z + d + NZ) % NZ) * NX + x}

    def at_h(d):
        return {"hist": (z + d[0]) % NZ * NX + (x + d[1]) % NX}

    def at_core():
        return {"row": 2 * y + 1 - core}

    def at_r(d):
        return {"row": (r + d) % NR}

    counts = {"send": 0, "recv": 0}
    pending = []

    def slots(kind, n):
        first = counts[kind]
        counts[kind] += n
        return first

    def copy(src, dst, send, recv, device):
        return pltpu.make_async_remote_copy(
            src_ref=src, dst_ref=dst, send_sem=send_sem.at[send], recv_sem=recv_sem.at[recv],
            device_id=device, device_id_type=MESH,
        )

    def start(cond, *args):
        if cond is None:
            copy(*args).start()
        else:
            @pl.when(cond)
            def _():
                copy(*args).start()

    def arrived(ref, recv):
        copy(ref, ref, 0, recv, at_x(1)).wait_recv()

    def drain():
        for cond, ref, send in pending:
            if cond is None:
                copy(ref, ref, send, 0, at_x(1)).wait_send()
            else:
                @pl.when(cond)
                def _():
                    copy(ref, ref, send, 0, at_x(1)).wait_send()
        pending.clear()

    def sent(cond, ref, send):
        pending.append((cond, ref, send))

    loads = []
    for src, dst in (
        (c_hbm, cv), (x_hbm, xv), (y_hbm, yv), (damp_hbm, dampv), (phase_hbm, phasev),
        (one_hbm, onev), (two_hbm, twov), (three_hbm, threev), (ret_hbm, retv), (les_hbm, lesv), (adv_hbm, advv),
    ):
        loads.append(pltpu.make_async_copy(src, dst, load_sem.at[len(loads)]))
        loads[-1].start()
    (c_load, x_load, y_load, damp_load, phase_load, one_load, two_load, three_load, ret_load, les_load, adv_load) = loads

    barrier = pltpu.get_barrier_semaphore()
    for d in range(1, NX):
        pl.semaphore_signal(barrier, inc=1, device_id=at_x(d), device_id_type=MESH)
    for d in range(1, NZ):
        pl.semaphore_signal(barrier, inc=1, device_id=at_z(d), device_id_type=MESH)
    for device in [at_r(d) for d in range(1, NR)]:
        pl.semaphore_signal(barrier, inc=1, device_id=device, device_id_type=MESH)
    for k, d in SPREAD.items():
        @pl.when((z - r + NZ) % NZ == d)
        def _():
            holder = (r // 2 + k // 2) % 4 * 2 + (r + k) % 2
            pl.semaphore_signal(barrier, inc=1, device_id={"hist": r * NX + x, "row": holder}, device_id_type=MESH)

    lane8 = lax.broadcasted_iota(jnp.int32, (8, 128), 1) // 32

    def by_group(parts):
        mask = lane8.reshape((1,) * (parts[0].ndim - 2) + (8, 128))
        out = parts[0]
        for g in range(1, 4):
            out = jnp.where(mask == g, parts[g], out)
        return out

    def rolled(a):
        flat = a.reshape(-1, 128)
        return [a] + [pltpu.roll(flat, 32 * d, 1).reshape(a.shape) for d in range(1, 4)]

    c_load.wait()
    coup = cv[...]
    wide = jnp.concatenate([coup] * 4, axis=1)
    square = jnp.concatenate([wide] * 4, axis=0)
    same = (
        lax.broadcasted_iota(jnp.int32, (128, 128), 0) // 32
        == lax.broadcasted_iota(jnp.int32, (128, 128), 1) // 32
    )
    right = jnp.where(same, square, 0.0)
    rows4 = [cv[pl.ds(g, 8, stride=4), :] for g in range(4)]
    col_of = [[jnp.broadcast_to(rows4[g][:, k : k + 1], (8, 128)) for k in range(32)] for g in range(4)]

    x_load.wait()
    y_load.wait()

    def part(ref, p):
        return ref[pl.ds(p, TP * 8, stride=2), :]

    xr, xi, yr, yi = part(xv, 0), part(xv, 1), part(yv, 0), part(yv, 1)
    polar = jnp.concatenate([-(xr * yr + xi * yi), -(xi * yr - xr * yi)], axis=0)
    half = lax.dot_general(polar, right, LANES_TO_LANES, precision=HIGHEST, preferred_element_type=F32)
    half = half.reshape(2 * TP, 8, 128)
    half_d = rolled(half)
    screen = jnp.zeros((2 * TP, 8, 128), F32)
    for d in range(4):
        for c in range(8):
            factor = by_group([col_of[g][4 * c + (g - d) % 4] for g in range(4)])
            screen = screen + factor[None] * half_d[d][:, c : c + 1, :]
    sr, si = screen[:TP], screen[TP:]
    xr, xi, yr, yi = (a.reshape(TP, 8, 128) for a in (xr, xi, yr, yi))
    less = (xr * sr - xi * si, xr * si + xi * sr)
    great = (yr * sr + yi * si, yi * sr - yr * si)
    ret = (great[0] - less[0], great[1] - less[1])
    less_d = [rolled(a) for a in less]
    for a, pair in enumerate(([rolled(v) for v in ret], less_d)):
        for p in range(2):
            for m in range(3):
                block = jnp.concatenate(
                    [by_group([pair[p][(g - b) % 4][4 * m + g] for g in range(4)]) for b in range(4)], axis=0
                )
                sig_own[a, pl.ds(p * 32, 32), pl.ds(m * 128, 128)] = block.astype(BF16)

    pl.semaphore_wait(barrier, (NX - 1) + (NZ - 1) + (NR - 1) + 1)

    z_send, z_recv = slots("send", 2), slots("recv", 4)
    for a in range(2):
        for half in range(2):
            rows = pl.ds(32 * half, 32)
            for k, d in SPREAD.items():
                if d == 0:
                    continue
                start(
                    (place == k) if a == 0 else (place == k) & ((z + d) % NZ > z),
                    sig_own.at[a, rows], sig_all.at[a, x, rows], z_send + a, z_recv + 2 * a + half,
                    {"hist": (z + d) % NZ * NX + x, "row": z},
                )

    @pl.when(source)
    def _():
        sig_all[:, x] = sig_own[...]

    sx_send, sx_recv = slots("send", 2), slots("recv", 2)
    sent(place != 5, sig_own.at[0], z_send)
    sent((place != 5) & goes_up, sig_own.at[1], z_send + 1)
    sent(None, sig_all.at[0, pl.ds(0, NX - 1)], sx_send)
    sent(late, sig_all.at[1, pl.ds(0, NX - 1)], sx_send + 1)

    def round_x(a, half, cond):
        block = sig_all.at[a, x, pl.ds(32 * half, 32)]
        for d in FAR_X:
            start(cond, block, block, sx_send + a, sx_recv + a, at_x(d))

    for a in range(2):
        for half in range(2):
            round_x(a, half, source)

    damp_load.wait()
    phase_load.wait()
    logs = jnp.concatenate([jnp.log(dampv[...]), phasev[...]], axis=1)
    tot = jnp.sum(logs, axis=0, keepdims=True)
    tot = jnp.concatenate([tot, jnp.zeros((1, 64), F32)], axis=1)
    tot_x[x] = jnp.broadcast_to(tot, (8, 128))

    tx_send, tx_recv = slots("send", 1), slots("recv", 1)
    sent(None, tot_z.at[pl.ds(0, NX - 1)], tx_send)
    for d in FAR_X:
        start(None, tot_x.at[x], tot_x.at[x], tx_send, tx_recv, at_x(d))

    @pl.when(early)
    def _():
        def square_of(p, s):
            rows = []
            for g in range(4):
                for b in range(4):
                    rows.append(jnp.where(lane8 == g, less_d[p][(g - b) % 4][s], 0.0))
            return jnp.concatenate(rows, axis=0)

        for s in range(TP):
            b0, b1 = square_of(0, s), square_of(1, s)
            bmat[s // 4, pl.ds(0, 128), pl.ds(s % 4 * 256, 128)] = b0.astype(BF16)
            bmat[s // 4, pl.ds(0, 128), pl.ds(s % 4 * 256 + 128, 128)] = b1.astype(BF16)
            bmat[s // 4, pl.ds(128, 128), pl.ds(s % 4 * 256, 128)] = (-b1).astype(BF16)
            bmat[s // 4, pl.ds(128, 128), pl.ds(s % 4 * 256 + 128, 128)] = b0.astype(BF16)

    weight = float(NX * NZ * TP * 32) ** -0.5
    ret_load.wait()
    three_load.wait()
    cx_send, cx_recv = slots("send", 1), slots("recv", 1)
    sent(early, col_x, cx_send)

    @pl.when(early)
    def _():
        t_row = lax.broadcasted_iota(jnp.int32, (TR, 128), 0)
        col_acc[...] = jnp.zeros_like(col_acc)

        def step(group, carry):
            rows = []
            for c in range(8):
                lanes = []
                for k in range(4):
                    at = group * 4 + k
                    keep = t_row >= h * TP + at - r * TR
                    for p in range(2):
                        lanes.append(jnp.where(keep, retv[p, at, :, pl.ds(c * 128, 128)], jnp.zeros((), BF16)))
                rows.append(jnp.concatenate(lanes, axis=1))
            col_acc[...] += lax.dot_general(
                jnp.concatenate(rows, axis=0), bmat[group], LANES_TO_LANES, preferred_element_type=F32
            )
            return carry

        lax.fori_loop(0, TP // 4, step, 0)
        for c in range(8):
            for po in range(2):
                value = (col_acc[pl.ds(c * TR, TR), pl.ds(po * 128, 128)] * -weight).astype(BF16)
                value = jnp.dot(value, threev[...], preferred_element_type=F32)
                col_send[c // 2, pl.ds(((c % 2) * 2 + po) * TR, TR), :] = value.astype(BF16)


    for a, cond in enumerate((jnp.logical_not(source), z > r)):
        for half in range(2):
            @pl.when(cond)
            def _():
                arrived(sig_own.at[a, pl.ds(0, 32)], z_recv + 2 * a + half)

            round_x(a, half, cond)

    for d in FAR_X:
        start(early, col_send.at[(x + d) % NX], col_x.at[d - 1], cx_send, cx_recv, at_x(d))

    tz_send, tz_recv = slots("send", 1), slots("recv", 1)
    sent(None, tot_z.at[pl.ds(0, NZ - 1)], tz_send)
    arrived(tot_x.at[pl.ds(0, NX - 1)], tx_recv)
    tot_z[z] = tot_x[0] + tot_x[1] + tot_x[2] + tot_x[3]
    for d in FAR_Z:
        start(None, tot_z.at[z], tot_z.at[z], tz_send, tz_recv, at_z(d))

    cz_send, cz_recv = slots("send", 1), slots("recv", 7)
    sent(early & (z < OWNERS), colz_send.at[pl.ds(0, OWNERS - 1)], cz_send)
    sent(early & (z >= OWNERS), colz_send, cz_send)

    @pl.when(early)
    def _():
        arrived(col_x, cx_recv)
        total = col_send[x].astype(F32)
        for d in range(1, NX):
            total = total + col_x[d - 1].astype(F32)
        for j in range(OWNERS):
            colz_send[j] = total[j * 32 : j * 32 + 32]

    for d in FAR_Z:
        to = (z + d) % NZ
        start(
            early & (to < OWNERS), colz_send.at[lax.rem(to, OWNERS)], col_z.at[d - 1], cz_send, cz_recv + d - 1, at_z(d)
        )

    one_load.wait()
    two_load.wait()

    def left_matrix(a):
        blocks = [
            jnp.dot(sig_all[a, j], onev[...], preferred_element_type=F32).astype(BF16) for j in range(NX)
        ]
        parts = []
        for p in range(2):
            gathered = jnp.concatenate(
                [
                    jnp.concatenate([b[p * 32 : p * 32 + 32, q * 128 : q * 128 + 128] for b in blocks], axis=1)
                    for q in range(4)
                ],
                axis=0,
            )
            parts.append(jnp.dot(gathered, twov[...], preferred_element_type=F32))
        lmat[pl.ds(0, 128), pl.ds(0, 384)] = parts[0].astype(BF16)
        lmat[pl.ds(0, 128), pl.ds(384, 384)] = (-parts[1]).astype(BF16)
        lmat[pl.ds(128, 128), pl.ds(0, 384)] = parts[1].astype(BF16)
        lmat[pl.ds(128, 128), pl.ds(384, 384)] = parts[0].astype(BF16)

    s_row = lax.broadcasted_iota(jnp.int32, (TR, 128), 0)

    def contract(ref, masked, half):
        def step(index, carry):
            pair = half * 3 + index
            cols = []
            for j in range(2):
                t = pair * 2 + j
                blocks = [ref[p, t, :, pl.ds(c * 128, 128)] for p in range(2) for c in range(8)]
                if masked:
                    keep = s_row <= h * TP + t - r * TR
                    blocks = [jnp.where(keep, b, jnp.zeros((), BF16)) for b in blocks]
                cols.append(jnp.concatenate(blocks, axis=0))
            out = jnp.dot(lmat[...], jnp.concatenate(cols, axis=1), preferred_element_type=F32) * weight
            for j in range(2):
                for po in range(2):
                    def block(q, b):
                        first = po * 128 + q * 32 + b * 8
                        return out[first : first + 8, j * 128 : j * 128 + 128]

                    total = by_group([block(q, q) for q in range(4)])
                    for d in range(1, 4):
                        moved = by_group([block(q, (q + d) % 4) for q in range(4)])
                        total = total + pltpu.roll(moved, 32 * d, 1)
                    at = (pair * 2 + j) * 2 + po
                    if masked:
                        fpart[at] += total
                    else:
                        fpart[at] = total
            return carry

        lax.fori_loop(0, TP // 4, step, 0, unroll=True)

    les_load.wait()
    arrived(sig_all.at[0, pl.ds(0, NX - 1)], sx_recv)
    left_matrix(0)
    contract(lesv, False, 1 - core)
    contract(lesv, False, core)
    adv_load.wait()

    @pl.when(late)
    def _():
        arrived(sig_all.at[1, pl.ds(0, NX - 1)], sx_recv + 1)
        left_matrix(1)
        contract(advv, True, 1 - core)

    rc_send, rc_recv = slots("send", 1), slots("recv", 1)
    sent(None, rs_buf, rc_send)
    start(None, fpart.at[pl.ds(TP * (1 - core), TP)], rs_buf, rc_send, rc_recv, at_core())

    @pl.when(late)
    def _():
        contract(advv, True, core)

    arrived(rs_buf, rc_recv)
    ry_send, ry_recv = slots("send", 1), slots("recv", 1)
    sent(None, y_buf.at[pl.ds(0, NR - 1)], ry_send)
    half = fpart[pl.ds(TP * core, TP)] + rs_buf[...]
    y_buf[r] = half.reshape(TP * 8, 128).astype(BF16)
    for d in FAR_R:
        start(None, y_buf.at[r], y_buf.at[r], ry_send, ry_recv, at_r(d))

    cg_send, cg_recv = slots("send", 1), slots("recv", 1)
    owner = z < OWNERS
    sent(owner, fpart.at[pl.ds(0, 14)], cg_send)

    @pl.when(owner)
    def _():
        @pl.when(early)
        def _():
            col_own[...] = colz_send[lax.rem(z, OWNERS)]

        @pl.when(jnp.logical_not(early))
        def _():
            col_own[...] = jnp.zeros_like(col_own)

        for d in range(1, NZ):
            @pl.when((z - d + NZ) % NZ <= r)
            def _():
                arrived(col_z.at[d - 1], cz_recv + d - 1)
                col_own[...] += col_z[d - 1]

        col_all[x, lax.rem(z, OWNERS)] = col_own[...].astype(BF16)

    piece = col_all.at[x, lax.rem(z, OWNERS)]
    for d in FAR_Z:
        start(owner, piece, piece, cg_send, cg_recv, at_z(d))

    arrived(tot_z.at[pl.ds(0, NZ - 1)], tz_recv)
    above = jnp.zeros((8, 128), F32)
    for j in range(NZ):
        above = above + jnp.where(j > z, tot_z[j], 0.0)
    for j in range(NX):
        above = above + jnp.where(j > x, tot_x[j], 0.0)
    row_i = lax.broadcasted_iota(jnp.int32, (TP, TP), 0)
    later = jnp.where(lax.broadcasted_iota(jnp.int32, (TP, TP), 1) >= row_i, 1.0, 0.0)
    summed = jnp.dot(later, logs, precision=HIGHEST, preferred_element_type=F32) + above[0:1, 0:64]
    magnitude = jnp.exp(summed[:, 0:32])
    angle = summed[:, 32:64]
    factor = jnp.concatenate([magnitude * jnp.cos(angle), -magnitude * jnp.sin(angle)], axis=0)
    spread = jnp.where(
        lax.broadcasted_iota(jnp.int32, (32, 1024), 1) // 32 == lax.broadcasted_iota(jnp.int32, (32, 1024), 0), 1.0, 0.0
    )
    spread = jnp.dot(factor, spread, precision=HIGHEST, preferred_element_type=F32)
    for c in range(8):
        facv[pl.ds(c, 2 * TP, stride=8), :] = spread[:, c * 128 : c * 128 + 128]

    arrived(y_buf.at[pl.ds(0, NR - 1)], ry_recv)
    halves = []
    for k in range(2):
        half = y_buf[k].astype(F32)
        for j in range(k + 2, NR, 2):
            half = half + y_buf[j].astype(F32)
        halves.append(half)

    squares = jnp.zeros((8, 128), F32)
    for t in range(TP):
        fr, fi = facv[pl.ds(t * 8, 8), :], facv[pl.ds((TP + t) * 8, 8), :]
        ar = xv[pl.ds(t * 16, 8, stride=2), :] + halves[t // 6][t % 6 * 16 : t % 6 * 16 + 8]
        ai = xv[pl.ds(t * 16 + 1, 8, stride=2), :] + halves[t // 6][t % 6 * 16 + 8 : t % 6 * 16 + 16]
        step_r, step_i = fr * ar - fi * ai, fr * ai + fi * ar
        stepv[2 * t] = step_r
        stepv[2 * t + 1] = step_i
        squares = squares + (step_r * step_r + step_i * step_i)
    norms[h] = jnp.sum(squares, axis=0, keepdims=True)
    n_send, n_recv = slots("send", 1), slots("recv", 1)
    for d in FAR_H:
        copy(norms.at[h], norms.at[h], n_send, n_recv, at_h(d)).start()

    ca_send, ca_recv = slots("send", 1), slots("recv", 1)
    sent(None, col_all.at[pl.ds(0, NX - 1)], ca_send)
    @pl.when(owner)
    def _():
        arrived(col_all.at[0, pl.ds(0, OWNERS - 1)], cg_recv)

    @pl.when(jnp.logical_not(owner))
    def _():
        arrived(col_all.at[0], cg_recv)

    for d in FAR_X:
        start(None, col_all.at[x], col_all.at[x], ca_send, ca_recv, at_x(d))

    arrived(col_all.at[pl.ds(0, NX - 1)], ca_recv)
    for j in range(NX):
        rows = col_all[j].reshape(4 * TR, 128)
        for c in range(2):
            for po in range(2):
                first = (2 * c + po) * TR
                col_ref[po, :, pl.ds((2 * j + c) * 128, 128)] = rows[first : first + TR]
    drain()

    others = norms.at[pl.ds(0, NH - 1)]
    copy(others, others, n_send, n_recv, at_x(1)).wait()
    total = jnp.sum(norms[...], axis=0)
    total = jnp.sum(total, axis=1, keepdims=True)
    scale = 1.0 / jnp.sqrt(total / float(2 * NX * NZ * TP * 1024) + 1e-6)
    for t in range(TP):
        out_ref[pl.ds(t * 16, 8, stride=2), :] = stepv[2 * t] * scale
        out_ref[pl.ds(t * 16 + 1, 8, stride=2), :] = stepv[2 * t + 1] * scale

    assert counts["send"] <= SENDS and counts["recv"] <= RECVS, counts


def finish(step_ref, col_ref, step_out, col_out, wide, sems):
    step = pltpu.make_async_copy(step_ref, step_out, sems.at[0])
    step.start()
    copies = []
    for p in range(2):
        wide[p] = col_ref[p].astype(F32)
        copies.append(pltpu.make_async_copy(wide.at[p], col_out.at[p], sems.at[1 + p]))
        copies[p].start()
    for copy in copies:
        copy.wait()
    step.wait()


SENDS = 13
RECVS = 21


def shards(row_less, row_great, coupling, damping, phases, lesser_hist, advanced_hist, retarded_hist):
    def rows(a):
        a = a.transpose(1, 0, 2).reshape(TP, 2, 8, 128)
        return a.transpose(0, 2, 1, 3).reshape(TP * 16, 128)

    one, two, three = (jnp.asarray(m, BF16) for m in lane_order())
    anywhere = pl.BlockSpec(memory_space=pltpu.HBM)
    vmem = pl.BlockSpec(memory_space=pltpu.VMEM)
    scratch = [
        pltpu.VMEM((TP * 16, 128), F32),
        pltpu.VMEM((TP * 16, 128), F32),
        pltpu.VMEM((32, 32), F32),
        pltpu.VMEM((TP, 32), F32),
        pltpu.VMEM((TP, 32), F32),
        pltpu.VMEM((2, TP, TR, 1024), BF16),
        pltpu.VMEM((2, TP, TR, 1024), BF16),
        pltpu.VMEM((2, TP, TR, 1024), BF16),
        pltpu.VMEM((TP * 32, 512), BF16),
        pltpu.VMEM((NX * 128, 8 * TR), BF16),
        pltpu.VMEM((128, 128), BF16),
        pltpu.VMEM((2, 64, TP * 32), BF16),
        pltpu.VMEM((2, NX, 64, TP * 32), BF16),
        pltpu.VMEM((TP // 4, 256, 1024), BF16),
        pltpu.VMEM((8 * TR, 256), F32),
        pltpu.VMEM((NX, 4 * TR, 128), BF16),
        pltpu.VMEM((NX - 1, 4 * TR, 128), BF16),
        pltpu.VMEM((OWNERS, 32, 128), F32),
        pltpu.VMEM((NZ - 1, 32, 128), F32),
        pltpu.VMEM((32, 128), F32),
        pltpu.VMEM((NX, OWNERS, 32, 128), BF16),
        pltpu.VMEM((256, 768), BF16),
        pltpu.VMEM((2 * TP, 8, 128), F32),
        pltpu.VMEM((TP, 8, 128), F32),
        pltpu.VMEM((NR, TP * 8, 128), BF16),
        pltpu.VMEM((NX, 8, 128), F32),
        pltpu.VMEM((NZ, 8, 128), F32),
        pltpu.VMEM((NH, 1, 128), F32),
        pltpu.VMEM((2 * TP * 8, 128), F32),
        pltpu.VMEM((2 * TP, 8, 128), F32),
        pltpu.SemaphoreType.DMA((11,)),
        pltpu.SemaphoreType.DMA((SENDS,)),
        pltpu.SemaphoreType.DMA((RECVS,)),
    ]
    operands = (
        rows(row_less), rows(row_great), coupling, damping, phases,
        lesser_hist.transpose(0, 2, 1, 3), advanced_hist.transpose(0, 2, 1, 3), retarded_hist.transpose(0, 2, 1, 3),
        one, two, three,
    )
    stepped, column = pl.pallas_call(
        body,
        out_shape=(
            jax.ShapeDtypeStruct((TP * 16, 128), F32),
            jax.ShapeDtypeStruct((2, TR, 1024), BF16),
        ),
        in_specs=[anywhere] * 11,
        out_specs=(vmem, vmem),
        scratch_shapes=scratch,
        compiler_params=pltpu.CompilerParams(
            collective_id=0, has_side_effects=True, vmem_limit_bytes=24 * 1024 * 1024
        ),
        name="kadanoff_baym_step",
    )(
        *(pltpu.with_memory_space_constraint(a, pltpu.HBM) for a in operands)
    )
    stepped, column = pl.pallas_call(
        finish,
        out_shape=(jax.ShapeDtypeStruct((TP * 16, 128), F32), jax.ShapeDtypeStruct((2, TR, 1024), F32)),
        in_specs=[vmem, vmem],
        out_specs=(pl.BlockSpec(memory_space=pltpu.HBM),) * 2,
        scratch_shapes=[pltpu.VMEM((2, TR, 1024), F32), pltpu.SemaphoreType.DMA((3,))],
        compiler_params=pltpu.CompilerParams(vmem_limit_bytes=4 * 1024 * 1024),
        name="finish",
    )(stepped, column)
    return stepped.reshape(TP, 8, 2, 128).transpose(2, 0, 1, 3).reshape(2, TP, 1024), column


def solution(mesh):
    return jax.shard_map(
        shards,
        mesh=mesh,
        in_specs=(
            P(None, "hist", None),
            P(None, "hist", None),
            P(),
            P("hist", None),
            P("hist", None),
            P(None, "row", "hist", None),
            P(None, "row", "hist", None),
            P(None, "row", "hist", None),
        ),
        out_specs=(P(None, "hist", None), P(None, "row", None)),
        check_vma=False,
    )
```
